512 devices in a mesh: group: 128 (over z, y, x_lo), bank: 4 (over x_hi, core).
Axes of the slice: x: 4 (x_hi: 2, x_lo: 2; x = x_hi * 2 + x_lo), y: 8, z: 8, core: 2. Of those that a mesh axis runs over, the one named last changes fastest.
Arguments:
- traces: bfloat16 [384, 131072], P('group'), may hold values from -127 to 127
- scales: float32 [384, 512], P('group'), may hold values from 0.004 to 0.04
- templates: bfloat16 [4, 128, 16, 128, 384], P('bank', 'group'), may hold values from -0.02734375 to 0.02734375
- owners: int32 [2, 4], P(None, 'bank'), may hold values from 0 to 127
Outputs:
- scores: float32 [2, 4, 16, 131072], P(None, 'bank', None, 'group')
- best_score: float32 [131072], P('group')
The draws below stay inside these ranges and needn't reach their ends.
All inputs are finite; a program needn't handle non-finite values.
Results may differ from the reference program's by a relative error of at most 0.0029.
Values may be sent and summed in bfloat16 or wider, within the bound.
No kernel may reach another device: no remote copies, remote signals or barrier semaphores. Data moves between devices by JAX's collectives and lax.ppermute only.
A program may use at most 128 MiB of HBM per device.

```python
import math
import jax
import jax.numpy as jnp
from jax import lax

TIME_DEV = 1024
TLEN = 128
TPL = 16
STEPS = 2
QB = 256
CH = 384
TOTAL = 131072
N_GROUP = 128
N_BANK = 4


def plant(result, own_key, least, high):
    shape = result.shape
    spot = [jax.random.randint(jax.random.fold_in(own_key, axis), (), 0, shape[axis]) for axis in range(len(shape))]
    result = result.at[tuple(spot)].set(least)
    longest = shape.index(max(shape))
    spot[longest] = (spot[longest] + 1) % shape[longest]
    return result.at[tuple(spot)].set(high)


def shard_levels(stream_key, extent, cuts, smallest, largest):
    level = 1.0
    for dim, shards_of in cuts:
        heights = jax.random.uniform(jax.random.fold_in(jax.random.fold_in(stream_key, 6), dim), (shards_of,), jnp.float32, smallest / len(cuts), largest / len(cuts))
        level = level * jnp.repeat(jnp.exp(heights), extent[dim] // shards_of).reshape((-1,) + (1,) * (len(extent) - 1 - dim))
    return level


def centred(key, dims, spread, most, cuts=(), kind=jnp.bfloat16):
    factor_of = shard_levels(key, dims, cuts, -0.22, 0.18) if cuts else 1.0
    drawn = jax.random.normal(key, dims, jnp.float32) * spread * factor_of
    return jnp.minimum(jnp.maximum(drawn, -most), most).astype(kind)


def setup_inputs(seed: int = 0) -> dict:
    key_list = jax.random.split(jax.random.key(seed), 5)
    traces = jnp.clip(jax.random.uniform(key_list[0], (CH, TOTAL), jnp.float32, -127.0, 127.0) * shard_levels(key_list[0], (CH, TOTAL), ((0, 128),), -0.4, 0.0), -127.0, 127.0).astype(jnp.bfloat16)
    scales = jnp.clip(jnp.exp(math.log(0.04) - 2.30258502 * jax.random.uniform(key_list[1], (CH, TOTAL // QB), jnp.float32) ** shard_levels(key_list[1], (CH, TOTAL // QB), ((0, 128),), -0.2, 0.2)), 0.004, 0.04)
    templates = centred(key_list[2], (N_BANK, N_GROUP, TPL, TLEN, CH), (CH * TLEN) ** -0.5, 0.02734375, ((0, 4), (1, 128)))
    owners = plant(jax.random.randint(key_list[3], (STEPS, N_BANK), 0, N_GROUP), jax.random.fold_in(key_list[3], 1), 0, N_GROUP - 1).astype(jnp.int32)
    return dict(traces=traces, scales=scales, templates=templates, owners=owners)


def reference(traces, scales, templates, owners):
    samples_all = traces.shape[1]
    blocked = traces.astype(jnp.float32).reshape(CH, scales.shape[1], -1)
    rounded = (blocked * scales[:, :, None]).reshape(CH, samples_all).astype(jnp.bfloat16)
    rounded = lax.optimization_barrier(rounded)
    signal = jnp.pad(rounded.astype(jnp.float32), ((0, 0), (0, TLEN)))
    fft_len = 1 << (TIME_DEV + TLEN).bit_length()
    n_blocks = samples_all // TIME_DEV
    bank_ids = jnp.arange(N_BANK, dtype=jnp.int32)
    results = []
    for step_idx in range(STEPS):
        chosen = templates[bank_ids, owners[step_idx]]
        kernel = chosen.astype(jnp.float32).transpose(0, 1, 3, 2).reshape(N_BANK * TPL, CH, TLEN)
        spectra = jnp.conj(jnp.fft.rfft(kernel, n=fft_len, axis=-1))

        def one_block(block_id, spectra=spectra):
            segment = lax.dynamic_slice_in_dim(signal, (block_id * TIME_DEV).astype(jnp.int32), TIME_DEV + TLEN, 1)
            data_spec = jnp.fft.rfft(segment, n=fft_len, axis=-1)
            summed = jnp.einsum("kcf,cf->kf", spectra, data_spec)
            return jnp.fft.irfft(summed, n=fft_len, axis=-1)[:, :TIME_DEV]

        pieces = lax.map(one_block, jnp.arange(n_blocks, dtype=jnp.int32))
        results.append(pieces.transpose(1, 0, 2).reshape(N_BANK, TPL, samples_all))
    scores = jnp.stack(results).astype(jnp.float32)
    best_score = jnp.max(scores, axis=(0, 1, 2))
    return scores, best_score
```

```python
import jax
import jax.numpy as jnp
from jax import lax
from jax.experimental import pallas as pl
from jax.experimental.pallas import tpu as pltpu
from jax.sharding import PartitionSpec as P

TLEN = 128
STEPS = 2
TPL = 16
CH = 384
TIME_DEV = 1024
LANES = 128

HI = 4
CUBES = 16
CLASSES = 8
STATION = 3
CLASS_CH = CUBES * STATION
SHIFTS = TLEN // 16
RUN_ROWS = 33
RUN = RUN_ROWS * LANES
SPAN = 4 * TIME_DEV
PIECE = TPL * CH // LANES
SAMPLE_ROWS = 208
SEND_ROWS = STEPS * PIECE + SAMPLE_ROWS
VMEM = pltpu.CompilerParams(vmem_limit_bytes=56 * 1024 * 1024)


def group_index(cube, klass):
    z_hi, y_hi = divmod(cube, HI)
    z_lo, low = divmod(klass, 4)
    return z_hi * 32 + z_lo * 16 + y_hi * 4 + low


CLASS_GROUPS = [[group_index(cube, klass) for cube in range(CUBES)] for klass in range(CLASSES)]
CUBE_GROUPS = [[group_index(cube, klass) for klass in range(CLASSES)] for cube in range(CUBES)]


def iota(shape, axis):
    return lax.broadcasted_iota(jnp.int32, shape, axis)


def matmul(left, right):
    return jnp.dot(left, right, preferred_element_type=jnp.float32)


def one_hot(flags):
    return jnp.where(flags, 1.0, 0.0).astype(jnp.bfloat16)


def split_kernel(block_ref, out_ref, sorted_ref):
    channel = iota((CH, 1), 0)
    station = channel // STATION
    cube = (station // 32) * HI + (station // 4) % HI
    klass = ((station // 16) % 2) * 4 + station % 4
    target = klass * LANES + (channel % STATION) * CUBES + cube
    by_class = one_hot(iota((CH, CLASSES * LANES), 1) == target)
    for shift in range(SHIFTS):
        rows = block_ref[:, shift * 16 : shift * 16 + 16, :].reshape(TPL * 16, CH)
        parted = matmul(rows, by_class).astype(jnp.bfloat16)
        for klass_id in range(CLASSES):
            sorted_ref[klass_id, :, shift * LANES : (shift + 1) * LANES] = parted[
                :, klass_id * LANES : (klass_id + 1) * LANES
            ]
    padded = iota((SHIFTS * LANES, 1), 0)
    lane = padded % LANES
    target = jnp.where(lane < CLASS_CH, (padded // LANES) * CLASS_CH + lane, -1)
    dense = one_hot(iota((SHIFTS * LANES, CH), 1) == target)
    for klass_id in range(CLASSES):
        packed = matmul(sorted_ref[klass_id], dense).astype(jnp.bfloat16)
        for cube_id in range(CUBES):
            for tile in range(CH // LANES):
                out_ref[group_index(cube_id, klass_id), tile * 16 : tile * 16 + 16, :] = packed[
                    cube_id * 16 : cube_id * 16 + 16, tile * LANES : (tile + 1) * LANES
                ]


def split_block(block):
    return pl.pallas_call(
        split_kernel,
        out_shape=jax.ShapeDtypeStruct((CUBES * CLASSES, PIECE, LANES), jnp.bfloat16),
        in_specs=[pl.BlockSpec(memory_space=pltpu.VMEM)],
        out_specs=pl.BlockSpec(memory_space=pltpu.VMEM),
        scratch_shapes=[pltpu.VMEM((CLASSES, TPL * 16, SHIFTS * LANES), jnp.bfloat16)],
        compiler_params=VMEM,
        cost_estimate=pl.CostEstimate(flops=3_200_000_000, bytes_accessed=3 << 20, transcendentals=0),
        name="split_block",
    )(block)


def pack_kernel(owners_ref, first_ref, second_ref, samples_ref, out_ref, wide_ref, stage_ref):
    wide_ref[:, 0:1024, :] = samples_ref[...].astype(jnp.float32)
    wide_ref[:, 1024:, :] = jnp.zeros((STATION, 8, LANES), jnp.float32)
    first = first_ref[0]
    second = second_ref[0]
    for cube in range(CUBES):
        z_hi, y_hi = divmod(cube, HI)
        out_ref[cube, 0:PIECE, :] = first
        out_ref[cube, PIECE : 2 * PIECE, :] = second
        for z_lo in range(2):
            for ch in range(STATION):
                start = z_hi * 256 + z_lo * 128 + y_hi * 32
                at = (z_lo * STATION + ch) * RUN_ROWS
                stage_ref[at : at + RUN_ROWS, :] = wide_ref[ch, start : start + RUN_ROWS, :]
        stage_ref[6 * RUN_ROWS :, :] = jnp.zeros((SAMPLE_ROWS - 6 * RUN_ROWS, LANES), jnp.float32)
        out_ref[cube, 2 * PIECE :, :] = stage_ref[...].astype(jnp.bfloat16)


def pack(owners, pieces, samples):
    spec = pltpu.PrefetchScalarGridSpec(
        num_scalar_prefetch=1,
        grid=(1,),
        in_specs=[
            pl.BlockSpec((1, PIECE, LANES), lambda i, owners: (owners[0], 0, 0)),
            pl.BlockSpec((1, PIECE, LANES), lambda i, owners: (owners[1], 0, 0)),
            pl.BlockSpec((STATION, 1024, LANES), lambda i, owners: (0, 0, 0)),
        ],
        out_specs=pl.BlockSpec((CUBES, SEND_ROWS, LANES), lambda i, owners: (0, 0, 0)),
        scratch_shapes=[
            pltpu.VMEM((STATION, 1032, LANES), jnp.float32),
            pltpu.VMEM((SAMPLE_ROWS, LANES), jnp.float32),
        ],
    )
    return pl.pallas_call(
        pack_kernel,
        grid_spec=spec,
        out_shape=jax.ShapeDtypeStruct((CUBES, SEND_ROWS, LANES), jnp.bfloat16),
        compiler_params=VMEM,
        cost_estimate=pl.CostEstimate(flops=1_000_000, bytes_accessed=2 << 20, transcendentals=0),
        name="pack",
    )(owners, pieces, pieces, samples)


def correlate_kernel(recv_ref, out_ref, stage_ref, natural_ref, weight_ref, x_ref, product_ref):
    for cube in range(CUBES):
        for step in range(STEPS):
            for tile in range(CH // LANES):
                at = step * PIECE + tile * 16
                natural_ref[(cube * STEPS + step) * 16 : (cube * STEPS + step + 1) * 16, tile * LANES : (tile + 1) * LANES] = (
                    recv_ref[cube, at : at + 16, :]
                )
        stage_ref[cube * SAMPLE_ROWS : (cube + 1) * SAMPLE_ROWS, :] = recv_ref[cube, 2 * PIECE :, :].astype(jnp.float32)
    rows = TPL * STEPS * 16
    wanted = iota((rows, 1), 0)
    lag, step, template = wanted // 32, (wanted // 16) % 2, wanted % 16
    order = one_hot(iota((rows, rows), 1) == (template * 2 + step) * 16 + lag)
    weight_ref[...] = matmul(order, natural_ref[...]).astype(jnp.bfloat16)
    for run in range(2):
        for ch in range(STATION):
            pieces = []
            for block in range(RUN_ROWS):
                at = (run * STATION + ch) * RUN_ROWS + block
                pieces.append(stage_ref[pl.ds(at, CUBES, stride=SAMPLE_ROWS), :])
            line = jnp.concatenate(pieces, axis=1)
            for shift in range(SHIFTS):
                moved = line if shift == 0 else pltpu.roll(line, RUN - 16 * shift, 1)
                at = shift * CLASS_CH + ch * CUBES
                x_ref[at : at + CUBES, :] = moved.astype(jnp.bfloat16)
        for start in range(0, RUN, 1408):
            product_ref[:, start : start + 1408] = matmul(weight_ref[...], x_ref[:, start : start + 1408])
        for part in range(4):
            total = product_ref[0:32, part * TIME_DEV : (part + 1) * TIME_DEV]
            for lag in range(1, 16):
                window = product_ref[lag * 32 : (lag + 1) * 32, part * TIME_DEV : (part + 1) * TIME_DEV + LANES]
                total = total + pltpu.roll(window, TIME_DEV + LANES - lag, 1)[:, :TIME_DEV]
            out_ref[run * 4 + part] = total


def correlate(received):
    return pl.pallas_call(
        correlate_kernel,
        out_shape=jax.ShapeDtypeStruct((CLASSES, STEPS * TPL, TIME_DEV), jnp.float32),
        in_specs=[pl.BlockSpec(memory_space=pltpu.VMEM)],
        out_specs=pl.BlockSpec(memory_space=pltpu.VMEM),
        scratch_shapes=[
            pltpu.VMEM((CUBES * SAMPLE_ROWS, LANES), jnp.float32),
            pltpu.VMEM((TPL * STEPS * 16, CH), jnp.bfloat16),
            pltpu.VMEM((TPL * STEPS * 16, CH), jnp.bfloat16),
            pltpu.VMEM((CH, RUN), jnp.bfloat16),
            pltpu.VMEM((TPL * STEPS * 16, RUN), jnp.float32),
        ],
        compiler_params=VMEM,
        cost_estimate=pl.CostEstimate(flops=3_400_000_000, bytes_accessed=3 << 20, transcendentals=0),
        name="correlate",
    )(received)


def body(traces, scales, templates, owners):
    station_ch, samples_all = traces.shape
    blocked = traces.astype(jnp.float32).reshape(station_ch, scales.shape[1], -1)
    samples = (blocked * scales[:, :, None]).astype(jnp.bfloat16).reshape(station_ch, samples_all // LANES, LANES)
    pieces = split_block(templates[0, 0])
    pieces = lax.all_to_all(pieces, "group", 0, 0, tiled=True)
    sent = pack(owners[:, 0], pieces, samples)
    received = lax.all_to_all(sent, "group", 0, 0, axis_index_groups=CLASS_GROUPS, tiled=True)
    partial = correlate(received)
    partial = lax.all_to_all(partial, "group", 0, 0, axis_index_groups=CUBE_GROUPS, tiled=True)
    scores = jnp.sum(partial, axis=0).reshape(STEPS, 1, TPL, TIME_DEV)
    best_score = lax.pmax(jnp.max(scores, axis=(0, 1, 2)), "bank")
    return (scores, best_score)


def solution(mesh):
    placed = (
        P("group", None),
        P("group", None),
        P("bank", "group", None, None, None),
        P(None, "bank"),
    )
    return jax.shard_map(
        body,
        mesh=mesh,
        in_specs=placed,
        out_specs=(P(None, "bank", None, "group"), P("group")),
        check_vma=False,
    )
```

```python
import jax
import jax.numpy as jnp
from jax import lax
from jax.experimental import pallas as pl
from jax.experimental.pallas import tpu as pltpu
from jax.sharding import PartitionSpec as P

TLEN = 128
STEPS = 2
TPL = 16
CH = 384
TIME_DEV = 1024
LANES = 128

HI = 4
CUBES = 16
CLASSES = 8
STATION = 3
CLASS_CH = CUBES * STATION
SHIFTS = TLEN // 16
RUN_ROWS = 33
RUN = RUN_ROWS * LANES
PIECE = TPL * CH // LANES
SAMPLE_ROWS = 112
SEND_ROWS = STEPS * PIECE + SAMPLE_ROWS
VMEM = pltpu.CompilerParams(vmem_limit_bytes=56 * 1024 * 1024)


def cube_of(group):
    return (group // 32) * HI + (group // 4) % HI


def class_of(group):
    return ((group // 16) % 2) * 4 + group % 4


def group_index(cube, klass):
    z_hi, y_hi = divmod(cube, HI)
    z_lo, low = divmod(klass, 4)
    return z_hi * 32 + z_lo * 16 + y_hi * 4 + low


CLASS_GROUPS = [[group_index(cube, klass) for cube in range(CUBES)] for klass in range(CLASSES)]
CUBE_GROUPS = [[group_index(cube, klass) for klass in range(CLASSES)] for cube in range(CUBES)]


def iota(shape, axis):
    return lax.broadcasted_iota(jnp.int32, shape, axis)


def matmul(left, right):
    return jnp.dot(left, right, preferred_element_type=jnp.float32)


def one_hot(flags):
    return jnp.where(flags, 1.0, 0.0).astype(jnp.bfloat16)


def split_kernel(block_ref, out_ref, moved_ref):
    channel = iota((CH, 1), 0)
    station = channel // STATION
    column = (channel % STATION) * CUBES + cube_of(station)
    klass = class_of(station)
    for shift in range(SHIFTS):
        rows = block_ref[:, shift * 16 : shift * 16 + 16, :].reshape(TPL * 16, CH)
        target = ((klass + shift) % CLASSES) * CLASS_CH + column
        moved_ref[shift] = matmul(rows, one_hot(iota((CH, CH), 1) == target)).astype(jnp.bfloat16)
    for klass in range(CLASSES):
        for tile in range(CH // LANES):
            lanes = slice(tile * LANES, (tile + 1) * LANES)
            slot_of_lane = (iota((1, LANES), 1) + tile * LANES) // CLASS_CH
            slots = range(tile * LANES // CLASS_CH, (tile * LANES + LANES - 1) // CLASS_CH + 1)
            packed = moved_ref[(slots[0] - klass) % CLASSES, :, lanes]
            for slot in slots[1:]:
                packed = jnp.where(slot_of_lane == slot, moved_ref[(slot - klass) % CLASSES, :, lanes], packed)
            for template in range(TPL):
                at = template * PIECE + tile * 16
                out_ref[klass, at : at + 16, :] = packed[template * 16 : template * 16 + 16]


def split_block(block):
    return pl.pallas_call(
        split_kernel,
        out_shape=jax.ShapeDtypeStruct((CLASSES, TPL * PIECE, LANES), jnp.bfloat16),
        in_specs=[pl.BlockSpec(memory_space=pltpu.VMEM)],
        out_specs=pl.BlockSpec(memory_space=pltpu.VMEM),
        scratch_shapes=[pltpu.VMEM((SHIFTS, TPL * 16, CH), jnp.bfloat16)],
        compiler_params=VMEM,
        cost_estimate=pl.CostEstimate(flops=1_000_000_000, bytes_accessed=3 << 20, transcendentals=0),
        name="split_block",
    )(block)


def pack_kernel(place_ref, first_ref, second_ref, samples_ref, out_ref, wide_ref, stage_ref):
    run = place_ref[0]
    wide_ref[:, 0:1024, :] = samples_ref[...].astype(jnp.float32)
    wide_ref[:, 1024:, :] = jnp.zeros((STATION, 8, LANES), jnp.float32)
    stage_ref[STATION * RUN_ROWS :, :] = jnp.zeros((SAMPLE_ROWS - STATION * RUN_ROWS, LANES), jnp.float32)
    for cube in range(CUBES):
        z_hi, y_hi = divmod(cube, HI)
        out_ref[cube, 0:PIECE, :] = first_ref[cube * PIECE : (cube + 1) * PIECE, :]
        out_ref[cube, PIECE : 2 * PIECE, :] = second_ref[cube * PIECE : (cube + 1) * PIECE, :]
        start = pl.multiple_of(run * 128 + (z_hi * 256 + y_hi * 32), 32)
        for ch in range(STATION):
            stage_ref[ch * RUN_ROWS : (ch + 1) * RUN_ROWS, :] = wide_ref[ch, pl.ds(start, RUN_ROWS), :]
        out_ref[cube, 2 * PIECE :, :] = stage_ref[...].astype(jnp.bfloat16)


def pack(place, first, second, samples):
    return pl.pallas_call(
        pack_kernel,
        out_shape=jax.ShapeDtypeStruct((CUBES, SEND_ROWS, LANES), jnp.bfloat16),
        in_specs=[pl.BlockSpec(memory_space=pltpu.SMEM)] + [pl.BlockSpec(memory_space=pltpu.VMEM)] * 3,
        out_specs=pl.BlockSpec(memory_space=pltpu.VMEM),
        scratch_shapes=[
            pltpu.VMEM((STATION, 1032, LANES), jnp.float32),
            pltpu.VMEM((SAMPLE_ROWS, LANES), jnp.float32),
        ],
        compiler_params=VMEM,
        cost_estimate=pl.CostEstimate(flops=1_000_000, bytes_accessed=2 << 20, transcendentals=0),
        name="pack",
    )(place, first, second, samples)


def line_up_kernel(received_ref, out_ref, stage_ref):
    for cube in range(CUBES):
        stage_ref[cube * SAMPLE_ROWS : (cube + 1) * SAMPLE_ROWS, :] = received_ref[cube, 2 * PIECE :, :].astype(jnp.float32)
    for ch in range(STATION):
        for block in range(RUN_ROWS):
            rows = stage_ref[pl.ds(ch * RUN_ROWS + block, CUBES, stride=SAMPLE_ROWS), :]
            out_ref[ch * CUBES : (ch + 1) * CUBES, block * LANES : (block + 1) * LANES] = rows.astype(jnp.bfloat16)


def line_up(received):
    return pl.pallas_call(
        line_up_kernel,
        out_shape=jax.ShapeDtypeStruct((CLASS_CH, RUN), jnp.bfloat16),
        in_specs=[pl.BlockSpec(memory_space=pltpu.VMEM)],
        out_specs=pl.BlockSpec(memory_space=pltpu.VMEM),
        scratch_shapes=[pltpu.VMEM((CUBES * SAMPLE_ROWS, LANES), jnp.float32)],
        compiler_params=VMEM,
        cost_estimate=pl.CostEstimate(flops=1_000_000, bytes_accessed=1 << 20, transcendentals=0),
        name="line_up",
    )(received)


def correlate_kernel(place_ref, own_ref, other_ref, pieces_ref, out_ref, natural_ref, weight_ref, x_ref, product_ref):
    own_run, klass = place_ref[0], place_ref[1]
    for template in range(TPL):
        for step in range(STEPS):
            row = (template * STEPS + step) * 16
            for tile in range(CH // LANES):
                at = step * PIECE + tile * 16
                natural_ref[row : row + 16, tile * LANES : (tile + 1) * LANES] = pieces_ref[template, at : at + 16, :]
    rows = TPL * STEPS * 16
    wanted = iota((rows, 1), 0)
    lag, step, template = wanted // 32, (wanted // 16) % 2, wanted % 16
    order = one_hot(iota((rows, rows), 1) == (template * 2 + step) * 16 + lag)
    weight_ref[...] = matmul(order, natural_ref[...]).astype(jnp.bfloat16)
    for run, line_ref in enumerate((own_ref, other_ref)):
        line = line_ref[...].astype(jnp.float32)
        for shift in range(SHIFTS):
            moved = line if shift == 0 else pltpu.roll(line, RUN - 16 * shift, 1)
            at = pl.multiple_of(((klass + shift) % CLASSES) * CLASS_CH, 16)
            x_ref[pl.ds(at, CLASS_CH), :] = moved.astype(jnp.bfloat16)
        for start in range(0, RUN, 1408):
            product_ref[:, start : start + 1408] = matmul(weight_ref[...], x_ref[:, start : start + 1408])
        first = (own_run if run == 0 else 1 - own_run) * 4
        for part in range(4):
            total = product_ref[0:32, part * TIME_DEV : (part + 1) * TIME_DEV]
            for lag in range(1, 16):
                window = product_ref[lag * 32 : (lag + 1) * 32, part * TIME_DEV : (part + 1) * TIME_DEV + LANES]
                total = total + pltpu.roll(window, TIME_DEV + LANES - lag, 1)[:, :TIME_DEV]
            out_ref[first + part] = total


def correlate(place, own, other, pieces):
    return pl.pallas_call(
        correlate_kernel,
        out_shape=jax.ShapeDtypeStruct((CLASSES, STEPS * TPL, TIME_DEV), jnp.float32),
        in_specs=[pl.BlockSpec(memory_space=pltpu.SMEM)] + [pl.BlockSpec(memory_space=pltpu.VMEM)] * 3,
        out_specs=pl.BlockSpec(memory_space=pltpu.VMEM),
        scratch_shapes=[
            pltpu.VMEM((TPL * STEPS * 16, CH), jnp.bfloat16),
            pltpu.VMEM((TPL * STEPS * 16, CH), jnp.bfloat16),
            pltpu.VMEM((CH, RUN), jnp.bfloat16),
            pltpu.VMEM((TPL * STEPS * 16, RUN), jnp.float32),
        ],
        compiler_params=VMEM,
        cost_estimate=pl.CostEstimate(flops=3_400_000_000, bytes_accessed=3 << 20, transcendentals=0),
        name="correlate",
    )(place, own, other, pieces)


def exchange(array, groups):
    return lax.all_to_all(array, "group", 0, 0, axis_index_groups=groups, tiled=True)


def body(traces, scales, templates, owners):
    station_ch, samples_all = traces.shape
    place = jnp.stack([lax.axis_index("bank") % 2, class_of(lax.axis_index("group"))]).astype(jnp.int32)
    blocked = traces.astype(jnp.float32).reshape(station_ch, scales.shape[1], -1)
    samples = (blocked * scales[:, :, None]).astype(jnp.bfloat16).reshape(station_ch, samples_all // LANES, LANES)
    by_class = exchange(split_block(templates[0, 0]), CUBE_GROUPS)
    near = [lax.dynamic_index_in_dim(by_class, class_of(owners[step, 0]), 0, keepdims=False) for step in range(STEPS)]
    received = exchange(pack(place, near[0], near[1], samples), CLASS_GROUPS)
    own = line_up(received)
    other = lax.ppermute(own, "bank", [(0, 1), (1, 0), (2, 3), (3, 2)])
    far = [
        lax.dynamic_slice(received, (cube_of(owners[step, 0]), step * PIECE, 0), (1, PIECE, LANES))
        for step in range(STEPS)
    ]
    piece = jnp.concatenate(far, axis=1)
    pieces = exchange(jnp.broadcast_to(piece, (CUBES, STEPS * PIECE, LANES)), CLASS_GROUPS)
    partial = exchange(correlate(place, own, other, pieces), CUBE_GROUPS)
    scores = jnp.sum(partial, axis=0).reshape(STEPS, 1, TPL, TIME_DEV)
    best_score = lax.pmax(jnp.max(scores, axis=(0, 1, 2)), "bank")
    return (scores, best_score)


def solution(mesh):
    placed = (
        P("group", None),
        P("group", None),
        P("bank", "group", None, None, None),
        P(None, "bank"),
    )
    return jax.shard_map(
        body,
        mesh=mesh,
        in_specs=placed,
        out_specs=(P(None, "bank", None, "group"), P("group")),
        check_vma=False,
    )
```

```python
import jax
import jax.numpy as jnp
from jax import lax
from jax.experimental import pallas as pl
from jax.experimental.pallas import tpu as pltpu
from jax.sharding import PartitionSpec as P

TLEN = 128
STEPS = 2
TPL = 16
CH = 384
TIME_DEV = 1024
LANES = 128

HI = 4
CUBES = 16
CLASSES = 8
STATION = 3
CLASS_CH = CUBES * STATION
SHIFTS = TLEN // 16
RUN_ROWS = 33
RUN = RUN_ROWS * LANES
PIECE = TPL * CH // LANES
SAMPLE_ROWS = 112
SEND_ROWS = STEPS * PIECE + SAMPLE_ROWS
CHUNKS = ((0, 1152), (1152, 2176), (2176, 3200), (3200, RUN))
LAGS = 8
DEPTH = TLEN // LAGS * CLASS_CH
ROWS = LAGS * STEPS * TPL


def vmem(mebibytes):
    return pltpu.CompilerParams(vmem_limit_bytes=mebibytes * 1024 * 1024)


def cube_of(group):
    return (group // 32) * HI + (group // 4) % HI


def class_of(group):
    return ((group // 16) % 2) * 4 + group % 4


def group_index(cube, klass):
    z_hi, y_hi = divmod(cube, HI)
    z_lo, low = divmod(klass, 4)
    return z_hi * 32 + z_lo * 16 + y_hi * 4 + low


CLASS_GROUPS = [[group_index(cube, klass) for cube in range(CUBES)] for klass in range(CLASSES)]
CUBE_GROUPS = [[group_index(cube, klass) for klass in range(CLASSES)] for cube in range(CUBES)]


def iota(shape, axis):
    return lax.broadcasted_iota(jnp.int32, shape, axis)


def matmul(left, right):
    return jnp.dot(left, right, preferred_element_type=jnp.float32)


def one_hot(flags):
    return jnp.where(flags, 1.0, 0.0).astype(jnp.bfloat16)


def split_kernel(block_ref, out_ref, moved_ref, packed_ref, sems):
    channel = iota((CH, 1), 0)
    station = channel // STATION
    column = (channel % STATION) * CUBES + cube_of(station)
    klass = class_of(station)
    for shift in range(SHIFTS):
        rows = block_ref[:, shift * 16 : shift * 16 + 16, :].reshape(TPL * 16, CH)
        target = ((klass + shift) % CLASSES) * CLASS_CH + column
        moved_ref[shift] = matmul(rows, one_hot(iota((CH, CH), 1) == target)).astype(jnp.bfloat16)
    copies = []
    for klass in range(CLASSES):
        for tile in range(CH // LANES):
            lanes = slice(tile * LANES, (tile + 1) * LANES)
            slot_of_lane = (iota((1, LANES), 1) + tile * LANES) // CLASS_CH
            slots = range(tile * LANES // CLASS_CH, (tile * LANES + LANES - 1) // CLASS_CH + 1)
            packed = moved_ref[(slots[0] - klass) % CLASSES, :, lanes]
            for slot in slots[1:]:
                packed = jnp.where(slot_of_lane == slot, moved_ref[(slot - klass) % CLASSES, :, lanes], packed)
            for template in range(TPL):
                at = template * PIECE + tile * 16
                packed_ref[klass, at : at + 16, :] = packed[template * 16 : template * 16 + 16]
        copies.append(pltpu.make_async_copy(packed_ref.at[klass], out_ref.at[klass], sems.at[klass]))
        copies[-1].start()
    for copy in copies:
        copy.wait()


def split_block(block):
    return pl.pallas_call(
        split_kernel,
        out_shape=pltpu.HBM((CLASSES, TPL * PIECE, LANES), jnp.bfloat16),
        in_specs=[pl.BlockSpec(memory_space=pltpu.VMEM)],
        out_specs=pl.BlockSpec(memory_space=pl.ANY),
        scratch_shapes=[
            pltpu.VMEM((SHIFTS, TPL * 16, CH), jnp.bfloat16),
            pltpu.VMEM((CLASSES, TPL * PIECE, LANES), jnp.bfloat16),
            pltpu.SemaphoreType.DMA((CLASSES,)),
        ],
        compiler_params=vmem(12),
        cost_estimate=pl.CostEstimate(flops=1_000_000_000, bytes_accessed=3 << 20, transcendentals=0),
        name="split_block",
    )(block)


def pack_kernel(place_ref, first_ref, second_ref, samples_ref, out_ref, wide_ref, stage_ref):
    run = place_ref[0]
    wide_ref[:, 0:1024, :] = samples_ref[...].astype(jnp.float32)
    wide_ref[:, 1024:, :] = jnp.zeros((STATION, 8, LANES), jnp.float32)
    stage_ref[STATION * RUN_ROWS :, :] = jnp.zeros((SAMPLE_ROWS - STATION * RUN_ROWS, LANES), jnp.float32)
    for cube in range(CUBES):
        z_hi, y_hi = divmod(cube, HI)
        out_ref[cube, 0:PIECE, :] = first_ref[cube * PIECE : (cube + 1) * PIECE, :]
        out_ref[cube, PIECE : 2 * PIECE, :] = second_ref[cube * PIECE : (cube + 1) * PIECE, :]
        start = pl.multiple_of(run * 128 + (z_hi * 256 + y_hi * 32), 32)
        for ch in range(STATION):
            stage_ref[ch * RUN_ROWS : (ch + 1) * RUN_ROWS, :] = wide_ref[ch, pl.ds(start, RUN_ROWS), :]
        out_ref[cube, 2 * PIECE :, :] = stage_ref[...].astype(jnp.bfloat16)


def pack(place, first, second, samples):
    return pl.pallas_call(
        pack_kernel,
        out_shape=jax.ShapeDtypeStruct((CUBES, SEND_ROWS, LANES), jnp.bfloat16),
        in_specs=[pl.BlockSpec(memory_space=pltpu.SMEM)] + [pl.BlockSpec(memory_space=pltpu.VMEM)] * 3,
        out_specs=pl.BlockSpec(memory_space=pltpu.VMEM),
        scratch_shapes=[
            pltpu.VMEM((STATION, 1032, LANES), jnp.float32),
            pltpu.VMEM((SAMPLE_ROWS, LANES), jnp.float32),
        ],
        compiler_params=vmem(8),
        cost_estimate=pl.CostEstimate(flops=1_000_000, bytes_accessed=2 << 20, transcendentals=0),
        name="pack",
    )(place, first, second, samples)


def line_up_kernel(received_ref, out_ref, stage_ref):
    for cube in range(CUBES):
        stage_ref[cube * SAMPLE_ROWS : (cube + 1) * SAMPLE_ROWS, :] = received_ref[cube, 2 * PIECE :, :].astype(jnp.float32)
    for ch in range(STATION):
        for block in range(RUN_ROWS):
            rows = stage_ref[pl.ds(ch * RUN_ROWS + block, CUBES, stride=SAMPLE_ROWS), :]
            out_ref[ch * CUBES : (ch + 1) * CUBES, block * LANES : (block + 1) * LANES] = rows.astype(jnp.bfloat16)


def line_up(received):
    return pl.pallas_call(
        line_up_kernel,
        out_shape=jax.ShapeDtypeStruct((CLASS_CH, RUN), jnp.bfloat16),
        in_specs=[pl.BlockSpec(memory_space=pltpu.VMEM)],
        out_specs=pl.BlockSpec(memory_space=pltpu.VMEM),
        scratch_shapes=[pltpu.VMEM((CUBES * SAMPLE_ROWS, LANES), jnp.float32)],
        compiler_params=vmem(8),
        cost_estimate=pl.CostEstimate(flops=1_000_000, bytes_accessed=1 << 20, transcendentals=0),
        name="line_up",
    )(received)


def correlate_kernel(
    place_ref, pieces_ref, own_ref, other_ref, out_ref, natural_ref, weight_ref, moved_ref, product_ref
):
    own_run, klass = place_ref[0], place_ref[1]
    for run, line_ref in enumerate((own_ref, other_ref)):
        line = line_ref[...]
        for odd in range(2):
            for shift in range(SHIFTS):
                by = 16 * shift + 8 * odd
                at = odd * CH + shift * CLASS_CH
                moved_ref[run, at : at + CLASS_CH, :] = pltpu.roll(line, RUN - by, 1) if by else line
    for template in range(TPL):
        for step in range(STEPS):
            row = (template * STEPS + step) * 16
            for tile in range(CH // LANES):
                at = step * PIECE + tile * 16
                natural_ref[row : row + 16, tile * LANES : (tile + 1) * LANES] = pieces_ref[template, at : at + 16, :]
    wanted = iota((2 * ROWS, 1), 0)
    lag, step, template = wanted // 32, (wanted // 16) % 2, wanted % 16
    order = one_hot(iota((2 * ROWS, 2 * ROWS), 1) == (template * 2 + step) * 16 + lag)
    ordered = pltpu.roll(matmul(order, natural_ref[...]), (CH - klass * CLASS_CH) % CH, 1).astype(jnp.bfloat16)
    weight_ref[:, 0:CH] = ordered[0:ROWS]
    weight_ref[:, CH:] = ordered[ROWS:]
    for run in range(2):
        first = (own_run if run == 0 else 1 - own_run) * 4
        for part, (start, stop) in enumerate(CHUNKS):
            product_ref[run, :, start:stop] = matmul(weight_ref[...], moved_ref[run, :, start:stop])
            at = part * TIME_DEV
            total = product_ref[run, 0:32, at : at + TIME_DEV]
            for lag in range(1, LAGS):
                window = product_ref[run, lag * 32 : (lag + 1) * 32, at : at + TIME_DEV + LANES]
                total = total + pltpu.roll(window, TIME_DEV + LANES - lag, 1)[:, :TIME_DEV]
            out_ref[first + part] = total


def correlate(place, pieces, own, other):
    return pl.pallas_call(
        correlate_kernel,
        out_shape=jax.ShapeDtypeStruct((CLASSES, STEPS * TPL, TIME_DEV), jnp.float32),
        in_specs=[pl.BlockSpec(memory_space=pltpu.SMEM)] + [pl.BlockSpec(memory_space=pltpu.VMEM)] * 3,
        out_specs=pl.BlockSpec(memory_space=pltpu.VMEM),
        scratch_shapes=[
            pltpu.VMEM((2 * ROWS, CH), jnp.bfloat16),
            pltpu.VMEM((ROWS, DEPTH), jnp.bfloat16),
            pltpu.VMEM((2, DEPTH, RUN), jnp.bfloat16),
            pltpu.VMEM((2, ROWS, RUN), jnp.float32),
        ],
        compiler_params=vmem(32),
        cost_estimate=pl.CostEstimate(flops=3_400_000_000, bytes_accessed=3 << 20, transcendentals=0),
        name="correlate",
    )(place, pieces, own, other)


def exchange(array, groups):
    return lax.all_to_all(array, "group", 0, 0, axis_index_groups=groups, tiled=True)


def body(traces, scales, templates, owners):
    station_ch, samples_all = traces.shape
    place = jnp.stack([lax.axis_index("bank") % 2, class_of(lax.axis_index("group"))]).astype(jnp.int32)
    blocked = traces.astype(jnp.float32).reshape(station_ch, scales.shape[1], -1)
    samples = (blocked * scales[:, :, None]).astype(jnp.bfloat16).reshape(station_ch, samples_all // LANES, LANES)
    by_class = exchange(split_block(templates[0, 0]), CUBE_GROUPS)
    near = [lax.dynamic_index_in_dim(by_class, class_of(owners[step, 0]), 0, keepdims=False) for step in range(STEPS)]
    received = exchange(pack(place, near[0], near[1], samples), CLASS_GROUPS)
    far = [
        lax.dynamic_slice(received, (cube_of(owners[step, 0]), step * PIECE, 0), (1, PIECE, LANES))
        for step in range(STEPS)
    ]
    piece = jnp.concatenate(far, axis=1)
    pieces = exchange(jnp.broadcast_to(piece, (CUBES, STEPS * PIECE, LANES)), CLASS_GROUPS)
    own = line_up(received)
    other = lax.ppermute(own, "bank", [(0, 1), (1, 0), (2, 3), (3, 2)])
    partial = exchange(correlate(place, pieces, own, other), CUBE_GROUPS)
    scores = jnp.sum(partial, axis=0).reshape(STEPS, 1, TPL, TIME_DEV)
    best_score = lax.pmax(jnp.max(scores, axis=(0, 1, 2)), "bank")
    return (scores, best_score)


def solution(mesh):
    placed = (
        P("group", None),
        P("group", None),
        P("bank", "group", None, None, None),
        P(None, "bank"),
    )
    return jax.shard_map(
        body,
        mesh=mesh,
        in_specs=placed,
        out_specs=(P(None, "bank", None, "group"), P("group")),
        check_vma=False,
    )
```

```python
import jax
import jax.numpy as jnp
from jax import lax
from jax.experimental import pallas as pl
from jax.experimental.pallas import tpu as pltpu
from jax.sharding import PartitionSpec as P

TLEN = 128
STEPS = 2
TPL = 16
CH = 384
TIME_DEV = 1024
LANES = 128

HI = 4
CUBES = 16
CLASSES = 8
STATION = 3
CLASS_CH = CUBES * STATION
SHIFTS = TLEN // 16
RUN_ROWS = 33
RUN = RUN_ROWS * LANES
PIECE = TPL * CH // LANES
HALF_ROWS = 17
HALF = HALF_ROWS * LANES
SAMPLE_ROWS = 64
SEND_ROWS = STEPS * PIECE + SAMPLE_ROWS
CHUNKS = ((0, 1152), (1152, 2176), (2176, 3200), (3200, RUN))
LAGS = 8
DEPTH = TLEN // LAGS * CLASS_CH
ROWS = LAGS * STEPS * TPL


def vmem(mebibytes):
    return pltpu.CompilerParams(vmem_limit_bytes=mebibytes * 1024 * 1024)


def cube_of(group):
    return ((group >> 5) << 2) | ((group >> 2) & 3)


def class_of(group):
    return ((group >> 2) & 4) | (group & 3)


def group_index(cube, klass):
    z_hi, y_hi = divmod(cube, HI)
    z_lo, low = divmod(klass, 4)
    return z_hi * 32 + z_lo * 16 + y_hi * 4 + low


CLASS_GROUPS = [[group_index(cube, klass) for cube in range(CUBES)] for klass in range(CLASSES)]
CUBE_GROUPS = [[group_index(cube, klass) for klass in range(CLASSES)] for cube in range(CUBES)]


def iota(shape, axis):
    return lax.broadcasted_iota(jnp.int32, shape, axis)


def matmul(left, right):
    return jnp.dot(left, right, preferred_element_type=jnp.float32)


def one_hot(flags):
    return jnp.where(flags, 1.0, 0.0).astype(jnp.bfloat16)


def split_kernel(block_ref, out_ref, moved_ref, packed_ref, sems):
    channel = iota((CH, 1), 0)
    station = channel // STATION
    column = (channel % STATION) * CUBES + cube_of(station)
    klass = class_of(station)
    for shift in range(SHIFTS):
        rows = block_ref[:, shift * 16 : shift * 16 + 16, :].reshape(TPL * 16, CH)
        target = ((klass + shift) % CLASSES) * CLASS_CH + column
        moved_ref[shift] = matmul(rows, one_hot(iota((CH, CH), 1) == target)).astype(jnp.bfloat16)
    copies = []
    for klass in range(CLASSES):
        for tile in range(CH // LANES):
            lanes = slice(tile * LANES, (tile + 1) * LANES)
            slot_of_lane = (iota((1, LANES), 1) + tile * LANES) // CLASS_CH
            slots = range(tile * LANES // CLASS_CH, (tile * LANES + LANES - 1) // CLASS_CH + 1)
            packed = moved_ref[(slots[0] - klass) % CLASSES, :, lanes]
            for slot in slots[1:]:
                packed = jnp.where(slot_of_lane == slot, moved_ref[(slot - klass) % CLASSES, :, lanes], packed)
            for template in range(TPL):
                at = template * PIECE + tile * 16
                packed_ref[klass, at : at + 16, :] = packed[template * 16 : template * 16 + 16]
        copies.append(pltpu.make_async_copy(packed_ref.at[klass], out_ref.at[klass], sems.at[klass]))
        copies[-1].start()
    for copy in copies:
        copy.wait()


def split_block(block):
    return pl.pallas_call(
        split_kernel,
        out_shape=pltpu.HBM((CLASSES, TPL * PIECE, LANES), jnp.bfloat16),
        in_specs=[pl.BlockSpec(memory_space=pltpu.VMEM)],
        out_specs=pl.BlockSpec(memory_space=pl.ANY),
        scratch_shapes=[
            pltpu.VMEM((SHIFTS, TPL * 16, CH), jnp.bfloat16),
            pltpu.VMEM((CLASSES, TPL * PIECE, LANES), jnp.bfloat16),
            pltpu.SemaphoreType.DMA((CLASSES,)),
        ],
        compiler_params=vmem(12),
        cost_estimate=pl.CostEstimate(flops=1_000_000_000, bytes_accessed=3 << 20, transcendentals=0),
        name="split_block",
    )(block)


def pack_kernel(place_ref, samples_ref, *refs):
    *near, out_ref, wide_ref, stage_ref = refs
    start_of_quarter = place_ref[0] * 128 + place_ref[2] * 16
    wide_ref[:, 0:1024, :] = samples_ref[...].astype(jnp.float32)
    wide_ref[:, 1024:, :] = jnp.zeros((STATION, 8, LANES), jnp.float32)
    stage_ref[STATION * HALF_ROWS :, :] = jnp.zeros((SAMPLE_ROWS - STATION * HALF_ROWS, LANES), jnp.float32)
    for cube in range(CUBES):
        z_hi, y_hi = divmod(cube, HI)
        for step, near_ref in enumerate(near):
            out_ref[cube, step * PIECE : (step + 1) * PIECE, :] = near_ref[cube * PIECE : (cube + 1) * PIECE, :]
        if not near:
            out_ref[cube, 0 : 2 * PIECE, :] = jnp.zeros((2 * PIECE, LANES), jnp.bfloat16)
        start = pl.multiple_of(start_of_quarter + (z_hi * 256 + y_hi * 32), 16)
        for ch in range(STATION):
            stage_ref[ch * HALF_ROWS : (ch + 1) * HALF_ROWS, :] = wide_ref[ch, pl.ds(start, HALF_ROWS), :]
        out_ref[cube, 2 * PIECE :, :] = stage_ref[...].astype(jnp.bfloat16)


def pack(place, samples, *near):
    return pl.pallas_call(
        pack_kernel,
        out_shape=jax.ShapeDtypeStruct((CUBES, SEND_ROWS, LANES), jnp.bfloat16),
        in_specs=[pl.BlockSpec(memory_space=pltpu.SMEM)] + [pl.BlockSpec(memory_space=pltpu.VMEM)] * (1 + len(near)),
        out_specs=pl.BlockSpec(memory_space=pltpu.VMEM),
        scratch_shapes=[
            pltpu.VMEM((STATION, 1032, LANES), jnp.float32),
            pltpu.VMEM((SAMPLE_ROWS, LANES), jnp.float32),
        ],
        compiler_params=vmem(8),
        cost_estimate=pl.CostEstimate(flops=1_000_000, bytes_accessed=2 << 20, transcendentals=0),
        name="pack",
    )(place, samples, *near)


def line_up_kernel(received_ref, out_ref, stage_ref):
    for cube in range(CUBES):
        stage_ref[cube * SAMPLE_ROWS : (cube + 1) * SAMPLE_ROWS, :] = received_ref[cube, 2 * PIECE :, :].astype(jnp.float32)
    for ch in range(STATION):
        for block in range(HALF_ROWS):
            rows = stage_ref[pl.ds(ch * HALF_ROWS + block, CUBES, stride=SAMPLE_ROWS), :]
            out_ref[ch * CUBES : (ch + 1) * CUBES, block * LANES : (block + 1) * LANES] = rows.astype(jnp.bfloat16)


def line_up(received):
    return pl.pallas_call(
        line_up_kernel,
        out_shape=jax.ShapeDtypeStruct((CLASS_CH, HALF), jnp.bfloat16),
        in_specs=[pl.BlockSpec(memory_space=pltpu.VMEM)],
        out_specs=pl.BlockSpec(memory_space=pltpu.VMEM),
        scratch_shapes=[pltpu.VMEM((CUBES * SAMPLE_ROWS, LANES), jnp.float32)],
        compiler_params=vmem(8),
        cost_estimate=pl.CostEstimate(flops=1_000_000, bytes_accessed=1 << 20, transcendentals=0),
        name="line_up",
    )(received)


def join_kernel(place_ref, own_ref, other_ref, out_ref):
    second = place_ref[2] == 1
    body = HALF - LANES

    @pl.when(second)
    def _():
        out_ref[:, 0:body] = other_ref[:, 0:body]
        out_ref[:, body:] = own_ref[...]

    @pl.when(jnp.logical_not(second))
    def _():
        out_ref[:, 0:body] = own_ref[:, 0:body]
        out_ref[:, body:] = other_ref[...]


def join(place, own, other):
    return pl.pallas_call(
        join_kernel,
        out_shape=jax.ShapeDtypeStruct((CLASS_CH, RUN), jnp.bfloat16),
        in_specs=[pl.BlockSpec(memory_space=pltpu.SMEM)] + [pl.BlockSpec(memory_space=pltpu.VMEM)] * 2,
        out_specs=pl.BlockSpec(memory_space=pltpu.VMEM),
        compiler_params=vmem(4),
        cost_estimate=pl.CostEstimate(flops=1_000_000, bytes_accessed=1 << 20, transcendentals=0),
        name="join",
    )(place, own, other)


def correlate_kernel(
    place_ref, pieces_ref, own_ref, other_ref, out_ref, natural_ref, weight_ref, moved_ref, product_ref
):
    own_run, klass = place_ref[0], place_ref[1]
    for run, line_ref in enumerate((own_ref, other_ref)):
        line = line_ref[...]
        for odd in range(2):
            for shift in range(SHIFTS):
                by = 16 * shift + 8 * odd
                at = odd * CH + shift * CLASS_CH
                moved_ref[run, at : at + CLASS_CH, :] = pltpu.roll(line, RUN - by, 1) if by else line
    for template in range(TPL):
        for step in range(STEPS):
            row = (template * STEPS + step) * 16
            for tile in range(CH // LANES):
                at = step * PIECE + tile * 16
                natural_ref[row : row + 16, tile * LANES : (tile + 1) * LANES] = pieces_ref[template, at : at + 16, :]
    wanted = iota((2 * ROWS, 1), 0)
    lag, step, template = wanted // 32, (wanted // 16) % 2, wanted % 16
    order = one_hot(iota((2 * ROWS, 2 * ROWS), 1) == (template * 2 + step) * 16 + lag)
    ordered = pltpu.roll(matmul(order, natural_ref[...]), (CH - klass * CLASS_CH) % CH, 1).astype(jnp.bfloat16)
    weight_ref[:, 0:CH] = ordered[0:ROWS]
    weight_ref[:, CH:] = ordered[ROWS:]
    for run in range(2):
        first = (own_run if run == 0 else 1 - own_run) * 4
        for part, (start, stop) in enumerate(CHUNKS):
            product_ref[run, :, start:stop] = matmul(weight_ref[...], moved_ref[run, :, start:stop])
            at = part * TIME_DEV
            total = product_ref[run, 0:32, at : at + TIME_DEV]
            for lag in range(1, LAGS):
                window = product_ref[run, lag * 32 : (lag + 1) * 32, at : at + TIME_DEV + LANES]
                total = total + pltpu.roll(window, TIME_DEV + LANES - lag, 1)[:, :TIME_DEV]
            out_ref[first + part] = total


def correlate(place, pieces, own, other):
    return pl.pallas_call(
        correlate_kernel,
        out_shape=jax.ShapeDtypeStruct((CLASSES, STEPS * TPL, TIME_DEV), jnp.float32),
        in_specs=[pl.BlockSpec(memory_space=pltpu.SMEM)] + [pl.BlockSpec(memory_space=pltpu.VMEM)] * 3,
        out_specs=pl.BlockSpec(memory_space=pltpu.VMEM),
        scratch_shapes=[
            pltpu.VMEM((2 * ROWS, CH), jnp.bfloat16),
            pltpu.VMEM((ROWS, DEPTH), jnp.bfloat16),
            pltpu.VMEM((2, DEPTH, RUN), jnp.bfloat16),
            pltpu.VMEM((2, ROWS, RUN), jnp.float32),
        ],
        compiler_params=vmem(32),
        cost_estimate=pl.CostEstimate(flops=3_400_000_000, bytes_accessed=3 << 20, transcendentals=0),
        name="correlate",
    )(place, pieces, own, other)


def exchange(array, groups):
    return lax.all_to_all(array, "group", 0, 0, axis_index_groups=groups, tiled=True)


def body(traces, scales, templates, owners):
    station_ch, samples_all = traces.shape
    group, bank = lax.axis_index("group"), lax.axis_index("bank")
    place = jnp.stack([bank & 1, class_of(group), bank >> 1]).astype(jnp.int32)
    owner = [owners[step, 0] for step in range(STEPS)]

    def scaled():
        blocked = traces.astype(jnp.float32).reshape(station_ch, scales.shape[1], -1)
        samples = (blocked * scales[:, :, None]).astype(jnp.bfloat16)
        return samples.reshape(station_ch, samples_all // LANES, LANES)

    def with_blocks():
        by_class = exchange(split_block(templates[0, 0]), CUBE_GROUPS)
        near = [lax.dynamic_index_in_dim(by_class, class_of(owner[step]), 0, keepdims=False) for step in range(STEPS)]
        return pack(place, scaled(), *near)

    def without_blocks():
        return pack(place, scaled())

    holds_owner = (cube_of(owner[0]) == cube_of(group)) | (cube_of(owner[1]) == cube_of(group))
    received = exchange(lax.cond(holds_owner, with_blocks, without_blocks), CLASS_GROUPS)
    far = [
        lax.dynamic_slice(received, (cube_of(owner[step]), step * PIECE, 0), (1, PIECE, LANES)) for step in range(STEPS)
    ]
    piece = jnp.concatenate(far, axis=1)
    pieces = exchange(jnp.broadcast_to(piece, (CUBES, STEPS * PIECE, LANES)), CLASS_GROUPS)
    half = line_up(received)
    own = join(place, half, lax.ppermute(half, "bank", [(0, 2), (2, 0), (1, 3), (3, 1)]))
    other = lax.ppermute(own, "bank", [(0, 1), (1, 0), (2, 3), (3, 2)])
    partial = exchange(correlate(place, pieces, own, other), CUBE_GROUPS)
    scores = jnp.sum(partial, axis=0).reshape(STEPS, 1, TPL, TIME_DEV)
    best_score = lax.pmax(jnp.max(scores, axis=(0, 1, 2)), "bank")
    return (scores, best_score)


def solution(mesh):
    placed = (
        P("group", None),
        P("group", None),
        P("bank", "group", None, None, None),
        P(None, "bank"),
    )
    return jax.shard_map(
        body,
        mesh=mesh,
        in_specs=placed,
        out_specs=(P(None, "bank", None, "group"), P("group")),
        check_vma=False,
    )
```

```python
import jax
import jax.numpy as jnp
from jax import lax
from jax.experimental import pallas as pl
from jax.experimental.pallas import tpu as pltpu
from jax.sharding import PartitionSpec as P

TLEN = 128
STEPS = 2
TPL = 16
CH = 384
TIME_DEV = 1024
LANES = 128

HI = 4
CUBES = 16
CLASSES = 8
STATION = 3
CLASS_CH = CUBES * STATION
SHIFTS = TLEN // 16
RUN_ROWS = 33
RUN = RUN_ROWS * LANES
PIECE = TPL * CH // LANES
HALF_ROWS = 17
HALF = HALF_ROWS * LANES
SAMPLE_ROWS = 64
CHUNKS = ((0, 1152), (1152, HALF))
LAGS = 8
DEPTH = TLEN // LAGS * CLASS_CH
ROWS = LAGS * STEPS * TPL


def vmem(mebibytes):
    return pltpu.CompilerParams(vmem_limit_bytes=mebibytes * 1024 * 1024)


def cube_of(group):
    return ((group >> 5) << 2) | ((group >> 2) & 3)


def class_of(group):
    return ((group >> 2) & 4) | (group & 3)


def group_index(cube, klass):
    z_hi, y_hi = divmod(cube, HI)
    z_lo, low = divmod(klass, 4)
    return z_hi * 32 + z_lo * 16 + y_hi * 4 + low


CLASS_GROUPS = [[group_index(cube, klass) for cube in range(CUBES)] for klass in range(CLASSES)]
CUBE_GROUPS = [[group_index(cube, klass) for klass in range(CLASSES)] for cube in range(CUBES)]


def iota(shape, axis):
    return lax.broadcasted_iota(jnp.int32, shape, axis)


def matmul(left, right):
    return jnp.dot(left, right, preferred_element_type=jnp.float32)


def in_hbm(array):
    return pltpu.with_memory_space_constraint(array, pltpu.HBM)


def one_hot(flags):
    return jnp.where(flags, 1.0, 0.0).astype(jnp.bfloat16)


def split_kernel(owners_ref, place_ref, block_ref, plan_ref, out_ref, rows_ref, order_ref, moved_ref, packed_ref, sems):
    loads = [
        pltpu.make_async_copy(block_ref.at[pl.ds(at, 4)], rows_ref.at[pl.ds(at, 4)], sems.at[CLASSES + at // 4])
        for at in range(0, TPL, 4)
    ]
    for load in loads:
        load.start()
    first, second, group = owners_ref[0, 0], owners_ref[0, 1], place_ref[1]
    plan_ref[1], plan_ref[2] = class_of(first), class_of(second)
    plan_ref[3], plan_ref[4] = cube_of(first), cube_of(second)
    here = cube_of(group)
    holds = jnp.where((cube_of(first) == here) | (cube_of(second) == here), 1, 0)
    plan_ref[0] = holds + jnp.where(cube_of(first) == cube_of(second), 2, 0)
    plan_ref[5] = jnp.where(cube_of(first) == here, class_of(first), class_of(second))
    channel = iota((CH, 1), 0)
    station = channel // STATION
    target = class_of(station) * CLASS_CH + (channel % STATION) * CUBES + cube_of(station)
    order_ref[...] = one_hot(iota((CH, CH), 1) == target)
    for part, load in enumerate(loads):
        load.wait()
        rows = rows_ref[part * 4 : part * 4 + 4].reshape(4 * TLEN, CH)
        sorted_rows = matmul(rows, order_ref[...]).astype(jnp.bfloat16).reshape(4, TLEN, CH)
        for shift in range(SHIFTS):
            lags = sorted_rows[:, shift * 16 : shift * 16 + 16, :].reshape(64, CH)
            moved_ref[shift, part * 64 : part * 64 + 64, :] = pltpu.roll(lags, shift * CLASS_CH, 1) if shift else lags
    copies = []
    for klass in range(CLASSES):
        for tile in range(CH // LANES):
            lanes = slice(tile * LANES, (tile + 1) * LANES)
            slot_of_lane = (iota((1, LANES), 1) + tile * LANES) // CLASS_CH
            slots = range(tile * LANES // CLASS_CH, (tile * LANES + LANES - 1) // CLASS_CH + 1)
            packed = moved_ref[(slots[0] - klass) % CLASSES, :, lanes]
            for slot in slots[1:]:
                packed = jnp.where(slot_of_lane == slot, moved_ref[(slot - klass) % CLASSES, :, lanes], packed)
            for template in range(TPL):
                at = template * PIECE + tile * 16
                packed_ref[klass, at : at + 16, :] = packed[template * 16 : template * 16 + 16]
        copies.append(pltpu.make_async_copy(packed_ref.at[klass], out_ref.at[klass], sems.at[klass]))
        copies[-1].start()
    for copy in copies:
        copy.wait()


def split_block(owners, place, block):
    return pl.pallas_call(
        split_kernel,
        out_shape=[
            jax.ShapeDtypeStruct((8,), jnp.int32),
            pltpu.HBM((CLASSES, TPL * PIECE, LANES), jnp.bfloat16),
        ],
        in_specs=[pl.BlockSpec(memory_space=pltpu.SMEM)] * 2 + [pl.BlockSpec(memory_space=pl.ANY)],
        out_specs=[pl.BlockSpec(memory_space=pltpu.SMEM), pl.BlockSpec(memory_space=pl.ANY)],
        scratch_shapes=[
            pltpu.VMEM((TPL, TLEN, CH), jnp.bfloat16),
            pltpu.VMEM((CH, CH), jnp.bfloat16),
            pltpu.VMEM((SHIFTS, TPL * 16, CH), jnp.bfloat16),
            pltpu.VMEM((CLASSES, TPL * PIECE, LANES), jnp.bfloat16),
            pltpu.SemaphoreType.DMA((CLASSES + 4,)),
        ],
        compiler_params=vmem(16),
        cost_estimate=pl.CostEstimate(flops=1_000_000_000, bytes_accessed=3 << 20, transcendentals=0),
        name="split_block",
    )(owners, place, in_hbm(block))


def pack_kernel(place_ref, samples_ref, out_ref, wide_ref, stage_ref):
    bank = place_ref[0]
    start_of_quarter = (bank & 1) * 128 + (bank >> 1) * 16
    wide_ref[:, 0:1024, :] = samples_ref[...].astype(jnp.float32)
    wide_ref[:, 1024:, :] = jnp.zeros((STATION, 8, LANES), jnp.float32)
    stage_ref[STATION * HALF_ROWS :, :] = jnp.zeros((SAMPLE_ROWS - STATION * HALF_ROWS, LANES), jnp.float32)
    for cube in range(CUBES):
        z_hi, y_hi = divmod(cube, HI)
        start = pl.multiple_of(start_of_quarter + (z_hi * 256 + y_hi * 32), 16)
        for ch in range(STATION):
            stage_ref[ch * HALF_ROWS : (ch + 1) * HALF_ROWS, :] = wide_ref[ch, pl.ds(start, HALF_ROWS), :]
        out_ref[cube] = stage_ref[...].astype(jnp.bfloat16)


def pack(place, samples):
    return pl.pallas_call(
        pack_kernel,
        out_shape=jax.ShapeDtypeStruct((CUBES, SAMPLE_ROWS, LANES), jnp.bfloat16),
        in_specs=[pl.BlockSpec(memory_space=pltpu.SMEM), pl.BlockSpec(memory_space=pltpu.VMEM)],
        out_specs=pl.BlockSpec(memory_space=pltpu.VMEM),
        scratch_shapes=[
            pltpu.VMEM((STATION, 1032, LANES), jnp.float32),
            pltpu.VMEM((SAMPLE_ROWS, LANES), jnp.float32),
        ],
        compiler_params=vmem(8),
        cost_estimate=pl.CostEstimate(flops=1_000_000, bytes_accessed=2 << 20, transcendentals=0),
        name="pack",
    )(place, samples)


def assemble_kernel(plan_ref, near_ref, rows_ref, out_ref):
    pieces = (out_ref.shape[1] - SAMPLE_ROWS) // PIECE
    for cube in range(CUBES):
        for at in range(pieces):
            out_ref[cube, at * PIECE : (at + 1) * PIECE, :] = near_ref[
                plan_ref[1 + at if pieces == STEPS else 5], cube * PIECE : (cube + 1) * PIECE, :
            ]
        out_ref[cube, pieces * PIECE :, :] = rows_ref[cube]


def assemble(pieces, plan, near, rows):
    return pl.pallas_call(
        assemble_kernel,
        out_shape=jax.ShapeDtypeStruct((CUBES, pieces * PIECE + SAMPLE_ROWS, LANES), jnp.bfloat16),
        in_specs=[pl.BlockSpec(memory_space=pltpu.SMEM)] + [pl.BlockSpec(memory_space=pltpu.VMEM)] * 2,
        out_specs=pl.BlockSpec(memory_space=pltpu.VMEM),
        compiler_params=vmem(8),
        cost_estimate=pl.CostEstimate(flops=1_000_000, bytes_accessed=2 << 20, transcendentals=0),
        name="assemble",
    )(plan, near, rows)


def line_up_kernel(plan_ref, received_ref, pieces_ref, out_ref, stage_ref):
    count = (received_ref.shape[1] - SAMPLE_ROWS) // PIECE
    for step in range(STEPS):
        at = step * PIECE if count == STEPS else 0
        piece = received_ref[plan_ref[3 + step], at : at + PIECE, :]
        for cube in range(CUBES):
            pieces_ref[cube, step * PIECE : (step + 1) * PIECE, :] = piece
    for cube in range(CUBES):
        stage_ref[cube * SAMPLE_ROWS : (cube + 1) * SAMPLE_ROWS, :] = received_ref[cube, count * PIECE :, :].astype(jnp.float32)
    for ch in range(STATION):
        for block in range(HALF_ROWS):
            rows = stage_ref[pl.ds(ch * HALF_ROWS + block, CUBES, stride=SAMPLE_ROWS), :]
            out_ref[ch * CUBES : (ch + 1) * CUBES, block * LANES : (block + 1) * LANES] = rows.astype(jnp.bfloat16)


def line_up(plan, received):
    return pl.pallas_call(
        line_up_kernel,
        out_shape=[
            jax.ShapeDtypeStruct((CUBES, STEPS * PIECE, LANES), jnp.bfloat16),
            jax.ShapeDtypeStruct((CLASS_CH, HALF), jnp.bfloat16),
        ],
        in_specs=[pl.BlockSpec(memory_space=pltpu.SMEM), pl.BlockSpec(memory_space=pltpu.VMEM)],
        out_specs=[pl.BlockSpec(memory_space=pltpu.VMEM)] * 2,
        scratch_shapes=[pltpu.VMEM((CUBES * SAMPLE_ROWS, LANES), jnp.float32)],
        compiler_params=vmem(8),
        cost_estimate=pl.CostEstimate(flops=1_000_000, bytes_accessed=2 << 20, transcendentals=0),
        name="line_up",
    )(plan, received)


def correlate_kernel(place_ref, pieces_ref, *refs):
    *lines, out_ref, natural_ref, weight_ref, moved_ref, product_ref = refs
    own_run, own_half, klass = place_ref[0] & 1, place_ref[0] >> 1, class_of(place_ref[1])
    for quarter, line_ref in enumerate(lines):
        line = line_ref[...]
        for odd in range(2):
            for shift in range(SHIFTS):
                by = 16 * shift + 8 * odd
                at = odd * CH + shift * CLASS_CH
                moved_ref[quarter, at : at + CLASS_CH, :] = pltpu.roll(line, HALF - by, 1) if by else line
    for template in range(TPL):
        for step in range(STEPS):
            row = (template * STEPS + step) * 16
            for tile in range(CH // LANES):
                at = step * PIECE + tile * 16
                natural_ref[row : row + 16, tile * LANES : (tile + 1) * LANES] = pieces_ref[template, at : at + 16, :]
    wanted = iota((2 * ROWS, 1), 0)
    lag, step, template = wanted // 32, (wanted // 16) % 2, wanted % 16
    order = one_hot(iota((2 * ROWS, 2 * ROWS), 1) == (template * 2 + step) * 16 + lag)
    ordered = pltpu.roll(matmul(order, natural_ref[...]), (CH - klass * CLASS_CH) % CH, 1).astype(jnp.bfloat16)
    weight_ref[:, 0:CH] = ordered[0:ROWS]
    weight_ref[:, CH:] = ordered[ROWS:]
    for quarter in range(4):
        first = (own_run ^ (quarter >> 1)) * 4 + (own_half ^ (quarter & 1)) * 2
        for part, (start, stop) in enumerate(CHUNKS):
            product_ref[quarter, :, start:stop] = matmul(weight_ref[...], moved_ref[quarter, :, start:stop])
            at = part * TIME_DEV
            total = product_ref[quarter, 0:32, at : at + TIME_DEV]
            for lag in range(1, LAGS):
                window = product_ref[quarter, lag * 32 : (lag + 1) * 32, at : at + TIME_DEV + LANES]
                total = total + pltpu.roll(window, TIME_DEV + LANES - lag, 1)[:, :TIME_DEV]
            out_ref[first + part] = total


def correlate(place, pieces, *lines):
    return pl.pallas_call(
        correlate_kernel,
        out_shape=jax.ShapeDtypeStruct((CLASSES, STEPS * TPL, TIME_DEV), jnp.float32),
        in_specs=[pl.BlockSpec(memory_space=pltpu.SMEM)] + [pl.BlockSpec(memory_space=pltpu.VMEM)] * 5,
        out_specs=pl.BlockSpec(memory_space=pltpu.VMEM),
        scratch_shapes=[
            pltpu.VMEM((2 * ROWS, CH), jnp.bfloat16),
            pltpu.VMEM((ROWS, DEPTH), jnp.bfloat16),
            pltpu.VMEM((4, DEPTH, HALF), jnp.bfloat16),
            pltpu.VMEM((4, ROWS, HALF), jnp.float32),
        ],
        compiler_params=vmem(32),
        cost_estimate=pl.CostEstimate(flops=3_400_000_000, bytes_accessed=3 << 20, transcendentals=0),
        name="correlate",
    )(place, pieces, *lines)


def exchange(array, groups):
    return lax.all_to_all(array, "group", 0, 0, axis_index_groups=groups, tiled=True)


def body(traces, scales, templates, owners):
    station_ch, samples_all = traces.shape
    place = jnp.stack([lax.axis_index("bank"), lax.axis_index("group")]).astype(jnp.int32)
    plan, by_class = split_block(owners.T, place, templates[0, 0])

    def sample_rows():
        blocked = traces.astype(jnp.float32).reshape(station_ch, scales.shape[1], -1)
        samples = (blocked * scales[:, :, None]).astype(jnp.bfloat16)
        return pack(place, samples.reshape(station_ch, samples_all // LANES, LANES))

    holds_owner, one_cube = (plan[0] & 1) == 1, plan[0] >= 2

    def from_cubes(count):
        def with_blocks():
            return assemble(count, plan, exchange(by_class, CUBE_GROUPS), sample_rows())

        def without_blocks():
            return jnp.pad(sample_rows(), ((0, 0), (count * PIECE, 0), (0, 0)))

        return line_up(plan, exchange(lax.cond(holds_owner, with_blocks, without_blocks), CLASS_GROUPS))

    piece, own = lax.cond(one_cube, lambda: from_cubes(2), lambda: from_cubes(1))
    halves, cores = [(0, 2), (2, 0), (1, 3), (3, 1)], [(0, 1), (1, 0), (2, 3), (3, 2)]
    other = lax.ppermute(own, "bank", halves)
    lines = [own, other, lax.ppermute(own, "bank", cores), lax.ppermute(other, "bank", cores)]
    pieces = exchange(piece, CLASS_GROUPS)
    partial = exchange(correlate(place, pieces, *lines), CUBE_GROUPS)
    scores = jnp.sum(partial, axis=0).reshape(STEPS, 1, TPL, TIME_DEV)
    best_score = lax.pmax(jnp.max(scores, axis=(0, 1, 2)), "bank")
    return (scores, best_score)


def solution(mesh):
    placed = (
        P("group", None),
        P("group", None),
        P("bank", "group", None, None, None),
        P(None, "bank"),
    )
    return jax.shard_map(
        body,
        mesh=mesh,
        in_specs=placed,
        out_specs=(P(None, "bank", None, "group"), P("group")),
        check_vma=False,
    )
```

```python
import jax
import jax.numpy as jnp
from jax import lax
from jax.experimental import pallas as pl
from jax.experimental.pallas import tpu as pltpu
from jax.sharding import PartitionSpec as P

TLEN = 128
STEPS = 2
TPL = 16
CH = 384
TIME_DEV = 1024
LANES = 128

HI = 4
CUBES = 16
CLASSES = 8
STATION = 3
CLASS_CH = CUBES * STATION
SHIFTS = TLEN // 16
RUN_ROWS = 33
RUN = RUN_ROWS * LANES
PIECE = TPL * CH // LANES
HALF_ROWS = 17
HALF = HALF_ROWS * LANES
SAMPLE_ROWS = 64
CHUNKS = ((0, 1152), (1152, HALF))
LAGS = 8
DEPTH = TLEN // LAGS * CLASS_CH
ROWS = LAGS * STEPS * TPL


def vmem(mebibytes):
    return pltpu.CompilerParams(vmem_limit_bytes=mebibytes * 1024 * 1024)


def cube_of(group):
    return ((group >> 5) << 2) | ((group >> 2) & 3)


def class_of(group):
    return ((group >> 2) & 4) | (group & 3)


def group_index(cube, klass):
    z_hi, y_hi = divmod(cube, HI)
    z_lo, low = divmod(klass, 4)
    return z_hi * 32 + z_lo * 16 + y_hi * 4 + low


CLASS_GROUPS = [[group_index(cube, klass) for cube in range(CUBES)] for klass in range(CLASSES)]
CUBE_GROUPS = [[group_index(cube, klass) for klass in range(CLASSES)] for cube in range(CUBES)]


def iota(shape, axis):
    return lax.broadcasted_iota(jnp.int32, shape, axis)


def matmul(left, right):
    return jnp.dot(left, right, preferred_element_type=jnp.float32)


def in_hbm(array):
    return pltpu.with_memory_space_constraint(array, pltpu.HBM)


def one_hot(flags):
    return jnp.where(flags, 1.0, 0.0).astype(jnp.bfloat16)


def split_kernel(
    owners_ref, block_ref, plan_ref, out_ref, owner_ref, rows_ref, order_ref, moved_ref, packed_ref, sems
):
    loads = [
        pltpu.make_async_copy(block_ref.at[pl.ds(at, 4)], rows_ref.at[pl.ds(at, 4)], sems.at[CLASSES + at // 4])
        for at in range(0, TPL, 4)
    ]
    for load in loads:
        load.start()
    group = lax.axis_index("group")
    read = pltpu.make_async_copy(owners_ref, owner_ref, sems.at[CLASSES + 4])
    read.start()
    read.wait()
    first, second = owner_ref[0, 0], owner_ref[0, 1]
    plan_ref[1], plan_ref[2] = class_of(first), class_of(second)
    plan_ref[3], plan_ref[4] = cube_of(first), cube_of(second)
    here = cube_of(group)
    holds = jnp.where((cube_of(first) == here) | (cube_of(second) == here), 1, 0)
    plan_ref[0] = holds + jnp.where(cube_of(first) == cube_of(second), 2, 0)
    plan_ref[5] = jnp.where(cube_of(first) == here, class_of(first), class_of(second))
    channel = iota((CH, 1), 0)
    station = channel // STATION
    target = class_of(station) * CLASS_CH + (channel % STATION) * CUBES + cube_of(station)
    order_ref[...] = one_hot(iota((CH, CH), 1) == target)
    for part, load in enumerate(loads):
        load.wait()
        rows = rows_ref[part * 4 : part * 4 + 4].reshape(4 * TLEN, CH)
        sorted_rows = matmul(rows, order_ref[...]).astype(jnp.bfloat16).reshape(4, TLEN, CH)
        for shift in range(SHIFTS):
            lags = sorted_rows[:, shift * 16 : shift * 16 + 16, :].reshape(64, CH)
            moved_ref[shift, part * 64 : part * 64 + 64, :] = pltpu.roll(lags, shift * CLASS_CH, 1) if shift else lags
    copies = []
    for klass in range(CLASSES):
        for tile in range(CH // LANES):
            lanes = slice(tile * LANES, (tile + 1) * LANES)
            slot_of_lane = (iota((1, LANES), 1) + tile * LANES) // CLASS_CH
            slots = range(tile * LANES // CLASS_CH, (tile * LANES + LANES - 1) // CLASS_CH + 1)
            packed = moved_ref[(slots[0] - klass) % CLASSES, :, lanes]
            for slot in slots[1:]:
                packed = jnp.where(slot_of_lane == slot, moved_ref[(slot - klass) % CLASSES, :, lanes], packed)
            for template in range(TPL):
                at = template * PIECE + tile * 16
                packed_ref[klass, at : at + 16, :] = packed[template * 16 : template * 16 + 16]
        copies.append(pltpu.make_async_copy(packed_ref.at[klass], out_ref.at[klass], sems.at[klass]))
        copies[-1].start()
    for copy in copies:
        copy.wait()


def split_block(owners, block):
    return pl.pallas_call(
        split_kernel,
        out_shape=[
            jax.ShapeDtypeStruct((8,), jnp.int32),
            pltpu.HBM((CLASSES, TPL * PIECE, LANES), jnp.bfloat16),
        ],
        in_specs=[pl.BlockSpec(memory_space=pl.ANY)] * 2,
        out_specs=[pl.BlockSpec(memory_space=pltpu.SMEM), pl.BlockSpec(memory_space=pl.ANY)],
        scratch_shapes=[
            pltpu.SMEM((1, STEPS), jnp.int32),
            pltpu.VMEM((TPL, TLEN, CH), jnp.bfloat16),
            pltpu.VMEM((CH, CH), jnp.bfloat16),
            pltpu.VMEM((SHIFTS, TPL * 16, CH), jnp.bfloat16),
            pltpu.VMEM((CLASSES, TPL * PIECE, LANES), jnp.bfloat16),
            pltpu.SemaphoreType.DMA((CLASSES + 5,)),
        ],
        compiler_params=vmem(16),
        cost_estimate=pl.CostEstimate(flops=1_000_000_000, bytes_accessed=3 << 20, transcendentals=0),
        name="split_block",
    )(in_hbm(owners), in_hbm(block))


def pack_kernel(samples_ref, out_ref, wide_ref, stage_ref):
    bank = lax.axis_index("bank")
    start_of_quarter = (bank & 1) * 128 + (bank >> 1) * 16
    wide_ref[:, 0:1024, :] = samples_ref[...].astype(jnp.float32)
    wide_ref[:, 1024:, :] = jnp.zeros((STATION, 8, LANES), jnp.float32)
    stage_ref[STATION * HALF_ROWS :, :] = jnp.zeros((SAMPLE_ROWS - STATION * HALF_ROWS, LANES), jnp.float32)
    for cube in range(CUBES):
        z_hi, y_hi = divmod(cube, HI)
        start = pl.multiple_of(start_of_quarter + (z_hi * 256 + y_hi * 32), 16)
        for ch in range(STATION):
            stage_ref[ch * HALF_ROWS : (ch + 1) * HALF_ROWS, :] = wide_ref[ch, pl.ds(start, HALF_ROWS), :]
        out_ref[cube] = stage_ref[...].astype(jnp.bfloat16)


def pack(samples):
    return pl.pallas_call(
        pack_kernel,
        out_shape=jax.ShapeDtypeStruct((CUBES, SAMPLE_ROWS, LANES), jnp.bfloat16),
        in_specs=[pl.BlockSpec(memory_space=pltpu.VMEM)],
        out_specs=pl.BlockSpec(memory_space=pltpu.VMEM),
        scratch_shapes=[
            pltpu.VMEM((STATION, 1032, LANES), jnp.float32),
            pltpu.VMEM((SAMPLE_ROWS, LANES), jnp.float32),
        ],
        compiler_params=vmem(8),
        cost_estimate=pl.CostEstimate(flops=1_000_000, bytes_accessed=2 << 20, transcendentals=0),
        name="pack",
    )(samples)


def assemble_kernel(plan_ref, near_ref, rows_ref, out_ref):
    pieces = (out_ref.shape[1] - SAMPLE_ROWS) // PIECE
    for cube in range(CUBES):
        for at in range(pieces):
            out_ref[cube, at * PIECE : (at + 1) * PIECE, :] = near_ref[
                plan_ref[1 + at if pieces == STEPS else 5], cube * PIECE : (cube + 1) * PIECE, :
            ]
        out_ref[cube, pieces * PIECE :, :] = rows_ref[cube]


def assemble(pieces, plan, near, rows):
    return pl.pallas_call(
        assemble_kernel,
        out_shape=jax.ShapeDtypeStruct((CUBES, pieces * PIECE + SAMPLE_ROWS, LANES), jnp.bfloat16),
        in_specs=[pl.BlockSpec(memory_space=pltpu.SMEM)] + [pl.BlockSpec(memory_space=pltpu.VMEM)] * 2,
        out_specs=pl.BlockSpec(memory_space=pltpu.VMEM),
        compiler_params=vmem(8),
        cost_estimate=pl.CostEstimate(flops=1_000_000, bytes_accessed=2 << 20, transcendentals=0),
        name="assemble",
    )(plan, near, rows)


def line_up_kernel(plan_ref, received_ref, pieces_ref, out_ref, stage_ref):
    count = (received_ref.shape[1] - SAMPLE_ROWS) // PIECE
    for step in range(STEPS):
        at = step * PIECE if count == STEPS else 0
        piece = received_ref[plan_ref[3 + step], at : at + PIECE, :]
        for cube in range(CUBES):
            pieces_ref[cube, step * PIECE : (step + 1) * PIECE, :] = piece
    for cube in range(CUBES):
        stage_ref[cube * SAMPLE_ROWS : (cube + 1) * SAMPLE_ROWS, :] = received_ref[cube, count * PIECE :, :].astype(jnp.float32)
    for ch in range(STATION):
        for block in range(HALF_ROWS):
            rows = stage_ref[pl.ds(ch * HALF_ROWS + block, CUBES, stride=SAMPLE_ROWS), :]
            out_ref[ch * CUBES : (ch + 1) * CUBES, block * LANES : (block + 1) * LANES] = rows.astype(jnp.bfloat16)


def line_up(plan, received):
    return pl.pallas_call(
        line_up_kernel,
        out_shape=[
            jax.ShapeDtypeStruct((CUBES, STEPS * PIECE, LANES), jnp.bfloat16),
            jax.ShapeDtypeStruct((CLASS_CH, HALF), jnp.bfloat16),
        ],
        in_specs=[pl.BlockSpec(memory_space=pltpu.SMEM), pl.BlockSpec(memory_space=pltpu.VMEM)],
        out_specs=[pl.BlockSpec(memory_space=pltpu.VMEM)] * 2,
        scratch_shapes=[pltpu.VMEM((CUBES * SAMPLE_ROWS, LANES), jnp.float32)],
        compiler_params=vmem(8),
        cost_estimate=pl.CostEstimate(flops=1_000_000, bytes_accessed=2 << 20, transcendentals=0),
        name="line_up",
    )(plan, received)


def correlate_kernel(pieces_ref, *refs):
    *lines, out_ref, natural_ref, weight_ref, moved_ref, product_ref = refs
    bank = lax.axis_index("bank")
    own_run, own_half, klass = bank & 1, bank >> 1, class_of(lax.axis_index("group"))
    for quarter, line_ref in enumerate(lines):
        line = line_ref[...]
        for odd in range(2):
            for shift in range(SHIFTS):
                by = 16 * shift + 8 * odd
                at = odd * CH + shift * CLASS_CH
                moved_ref[quarter, at : at + CLASS_CH, :] = pltpu.roll(line, HALF - by, 1) if by else line
    for template in range(TPL):
        for step in range(STEPS):
            row = (template * STEPS + step) * 16
            for tile in range(CH // LANES):
                at = step * PIECE + tile * 16
                natural_ref[row : row + 16, tile * LANES : (tile + 1) * LANES] = pieces_ref[template, at : at + 16, :]
    wanted = iota((2 * ROWS, 1), 0)
    lag, step, template = wanted // 32, (wanted // 16) % 2, wanted % 16
    order = one_hot(iota((2 * ROWS, 2 * ROWS), 1) == (template * 2 + step) * 16 + lag)
    ordered = pltpu.roll(matmul(order, natural_ref[...]), (CH - klass * CLASS_CH) % CH, 1).astype(jnp.bfloat16)
    weight_ref[:, 0:CH] = ordered[0:ROWS]
    weight_ref[:, CH:] = ordered[ROWS:]
    for quarter in range(4):
        first = (own_run ^ (quarter >> 1)) * 4 + (own_half ^ (quarter & 1)) * 2
        for part, (start, stop) in enumerate(CHUNKS):
            product_ref[quarter, :, start:stop] = matmul(weight_ref[...], moved_ref[quarter, :, start:stop])
            at = part * TIME_DEV
            total = product_ref[quarter, 0:32, at : at + TIME_DEV]
            for lag in range(1, LAGS):
                window = product_ref[quarter, lag * 32 : (lag + 1) * 32, at : at + TIME_DEV + LANES]
                total = total + pltpu.roll(window, TIME_DEV + LANES - lag, 1)[:, :TIME_DEV]
            out_ref[first + part] = total


def correlate(pieces, *lines):
    return pl.pallas_call(
        correlate_kernel,
        out_shape=jax.ShapeDtypeStruct((CLASSES, STEPS * TPL, TIME_DEV), jnp.float32),
        in_specs=[pl.BlockSpec(memory_space=pltpu.VMEM)] * 5,
        out_specs=pl.BlockSpec(memory_space=pltpu.VMEM),
        scratch_shapes=[
            pltpu.VMEM((2 * ROWS, CH), jnp.bfloat16),
            pltpu.VMEM((ROWS, DEPTH), jnp.bfloat16),
            pltpu.VMEM((4, DEPTH, HALF), jnp.bfloat16),
            pltpu.VMEM((4, ROWS, HALF), jnp.float32),
        ],
        compiler_params=vmem(32),
        cost_estimate=pl.CostEstimate(flops=3_400_000_000, bytes_accessed=3 << 20, transcendentals=0),
        name="correlate",
    )(pieces, *lines)


def exchange(array, groups):
    return lax.all_to_all(array, "group", 0, 0, axis_index_groups=groups, tiled=True)


def body(traces, scales, templates, owners):
    station_ch, samples_all = traces.shape
    plan, by_class = split_block(owners.T, templates[0, 0])

    def sample_rows():
        blocked = traces.astype(jnp.float32).reshape(station_ch, scales.shape[1], -1)
        samples = (blocked * scales[:, :, None]).astype(jnp.bfloat16)
        return pack(samples.reshape(station_ch, samples_all // LANES, LANES))

    holds_owner, one_cube = (plan[0] & 1) == 1, plan[0] >= 2

    def from_cubes(count):
        def with_blocks():
            return assemble(count, plan, exchange(by_class, CUBE_GROUPS), sample_rows())

        def without_blocks():
            return jnp.pad(sample_rows(), ((0, 0), (count * PIECE, 0), (0, 0)))

        return line_up(plan, exchange(lax.cond(holds_owner, with_blocks, without_blocks), CLASS_GROUPS))

    piece, own = lax.cond(one_cube, lambda: from_cubes(2), lambda: from_cubes(1))
    halves, cores = [(0, 2), (2, 0), (1, 3), (3, 1)], [(0, 1), (1, 0), (2, 3), (3, 2)]
    other = lax.ppermute(own, "bank", halves)
    lines = [own, other, lax.ppermute(own, "bank", cores), lax.ppermute(other, "bank", cores)]
    pieces = exchange(piece, CLASS_GROUPS)
    partial = exchange(correlate(pieces, *lines), CUBE_GROUPS)
    scores = jnp.sum(partial, axis=0).reshape(STEPS, 1, TPL, TIME_DEV)
    best_score = lax.pmax(jnp.max(scores, axis=(0, 1, 2)), "bank")
    return (scores, best_score)


def solution(mesh):
    placed = (
        P("group", None),
        P("group", None),
        P("bank", "group", None, None, None),
        P(None, "bank"),
    )
    return jax.shard_map(
        body,
        mesh=mesh,
        in_specs=placed,
        out_specs=(P(None, "bank", None, "group"), P("group")),
        check_vma=False,
    )
```

```python
import jax
import jax.numpy as jnp
from jax import lax
from jax.experimental import pallas as pl
from jax.experimental.pallas import tpu as pltpu
from jax.sharding import PartitionSpec as P

TLEN = 128
STEPS = 2
TPL = 16
CH = 384
TIME_DEV = 1024
LANES = 128

HI = 4
CUBES = 16
CLASSES = 8
STATION = 3
CLASS_CH = CUBES * STATION
SHIFTS = TLEN // 16
RUN_ROWS = 33
RUN = RUN_ROWS * LANES
PIECE = TPL * CH // LANES
HALF_ROWS = 17
HALF = HALF_ROWS * LANES
SAMPLE_ROWS = 64
CHUNKS = ((0, 1152), (1152, HALF))
LAGS = 8
DEPTH = TLEN // LAGS * CLASS_CH
ROWS = LAGS * STEPS * TPL


def vmem(mebibytes):
    return pltpu.CompilerParams(vmem_limit_bytes=mebibytes * 1024 * 1024)


def cube_of(group):
    return ((group >> 5) << 2) | ((group >> 2) & 3)


def class_of(group):
    return ((group >> 2) & 4) | (group & 3)


def group_index(cube, klass):
    z_hi, y_hi = divmod(cube, HI)
    z_lo, low = divmod(klass, 4)
    return z_hi * 32 + z_lo * 16 + y_hi * 4 + low


CLASS_GROUPS = [[group_index(cube, klass) for cube in range(CUBES)] for klass in range(CLASSES)]
CUBE_GROUPS = [[group_index(cube, klass) for klass in range(CLASSES)] for cube in range(CUBES)]


def iota(shape, axis):
    return lax.broadcasted_iota(jnp.int32, shape, axis)


def matmul(left, right):
    return jnp.dot(left, right, preferred_element_type=jnp.float32)


def in_hbm(array):
    return pltpu.with_memory_space_constraint(array, pltpu.HBM)


def one_hot(flags):
    return jnp.where(flags, 1.0, 0.0).astype(jnp.bfloat16)


def split_kernel(
    owners_ref, block_ref, plan_ref, out_ref, owner_ref, rows_ref, order_ref, moved_ref, packed_ref, sems
):
    loads = [
        pltpu.make_async_copy(block_ref.at[pl.ds(at, 4)], rows_ref.at[pl.ds(at, 4)], sems.at[CLASSES + at // 4])
        for at in range(0, TPL, 4)
    ]
    for load in loads:
        load.start()
    group = lax.axis_index("group")
    read = pltpu.make_async_copy(owners_ref, owner_ref, sems.at[CLASSES + 4])
    read.start()
    read.wait()
    first, second = owner_ref[0, 0], owner_ref[0, 1]
    plan_ref[1], plan_ref[2] = class_of(first), class_of(second)
    plan_ref[3], plan_ref[4] = cube_of(first), cube_of(second)
    here = cube_of(group)
    holds = jnp.where((cube_of(first) == here) | (cube_of(second) == here), 1, 0)
    plan_ref[0] = holds + jnp.where(cube_of(first) == cube_of(second), 2, 0)
    plan_ref[5] = jnp.where(cube_of(first) == here, class_of(first), class_of(second))
    channel = iota((CH, 1), 0)
    station = channel // STATION
    target = class_of(station) * CLASS_CH + (channel % STATION) * CUBES + cube_of(station)
    order_ref[...] = one_hot(iota((CH, CH), 1) == target)
    for part, load in enumerate(loads):
        load.wait()
        rows = rows_ref[part * 4 : part * 4 + 4].reshape(4 * TLEN, CH)
        sorted_rows = matmul(rows, order_ref[...]).astype(jnp.bfloat16).reshape(4, TLEN, CH)
        for shift in range(SHIFTS):
            lags = sorted_rows[:, shift * 16 : shift * 16 + 16, :].reshape(64, CH)
            moved_ref[shift, part * 64 : part * 64 + 64, :] = pltpu.roll(lags, shift * CLASS_CH, 1) if shift else lags
    copies = []
    for klass in range(CLASSES):
        for tile in range(CH // LANES):
            lanes = slice(tile * LANES, (tile + 1) * LANES)
            slot_of_lane = (iota((1, LANES), 1) + tile * LANES) // CLASS_CH
            slots = range(tile * LANES // CLASS_CH, (tile * LANES + LANES - 1) // CLASS_CH + 1)
            packed = moved_ref[(slots[0] - klass) % CLASSES, :, lanes]
            for slot in slots[1:]:
                packed = jnp.where(slot_of_lane == slot, moved_ref[(slot - klass) % CLASSES, :, lanes], packed)
            for template in range(TPL):
                at = template * PIECE + tile * 16
                packed_ref[klass, at : at + 16, :] = packed[template * 16 : template * 16 + 16]
        copies.append(pltpu.make_async_copy(packed_ref.at[klass], out_ref.at[klass], sems.at[klass]))
        copies[-1].start()
    for copy in copies:
        copy.wait()


def split_block(owners, block):
    return pl.pallas_call(
        split_kernel,
        out_shape=[
            jax.ShapeDtypeStruct((8,), jnp.int32),
            pltpu.HBM((CLASSES, TPL * PIECE, LANES), jnp.bfloat16),
        ],
        in_specs=[pl.BlockSpec(memory_space=pl.ANY)] * 2,
        out_specs=[pl.BlockSpec(memory_space=pltpu.SMEM), pl.BlockSpec(memory_space=pl.ANY)],
        scratch_shapes=[
            pltpu.SMEM((1, STEPS), jnp.int32),
            pltpu.VMEM((TPL, TLEN, CH), jnp.bfloat16),
            pltpu.VMEM((CH, CH), jnp.bfloat16),
            pltpu.VMEM((SHIFTS, TPL * 16, CH), jnp.bfloat16),
            pltpu.VMEM((CLASSES, TPL * PIECE, LANES), jnp.bfloat16),
            pltpu.SemaphoreType.DMA((CLASSES + 5,)),
        ],
        compiler_params=vmem(16),
        cost_estimate=pl.CostEstimate(flops=1_000_000_000, bytes_accessed=3 << 20, transcendentals=0),
        name="split_block",
    )(in_hbm(owners), in_hbm(block))


def pack_kernel(samples_ref, out_ref, wide_ref, stage_ref):
    bank = lax.axis_index("bank")
    start_of_quarter = (bank & 1) * 128 + (bank >> 1) * 16
    wide_ref[:, 0:1024, :] = samples_ref[...].astype(jnp.float32)
    wide_ref[:, 1024:, :] = jnp.zeros((STATION, 8, LANES), jnp.float32)
    stage_ref[STATION * HALF_ROWS :, :] = jnp.zeros((SAMPLE_ROWS - STATION * HALF_ROWS, LANES), jnp.float32)
    for cube in range(CUBES):
        z_hi, y_hi = divmod(cube, HI)
        start = pl.multiple_of(start_of_quarter + (z_hi * 256 + y_hi * 32), 16)
        for ch in range(STATION):
            stage_ref[ch * HALF_ROWS : (ch + 1) * HALF_ROWS, :] = wide_ref[ch, pl.ds(start, HALF_ROWS), :]
        out_ref[cube] = stage_ref[...].astype(jnp.bfloat16)


def pack(samples):
    return pl.pallas_call(
        pack_kernel,
        out_shape=jax.ShapeDtypeStruct((CUBES, SAMPLE_ROWS, LANES), jnp.bfloat16),
        in_specs=[pl.BlockSpec(memory_space=pltpu.VMEM)],
        out_specs=pl.BlockSpec(memory_space=pltpu.VMEM),
        scratch_shapes=[
            pltpu.VMEM((STATION, 1032, LANES), jnp.float32),
            pltpu.VMEM((SAMPLE_ROWS, LANES), jnp.float32),
        ],
        compiler_params=vmem(8),
        cost_estimate=pl.CostEstimate(flops=1_000_000, bytes_accessed=2 << 20, transcendentals=0),
        name="pack",
    )(samples)


def assemble_kernel(plan_ref, near_ref, rows_ref, out_ref):
    pieces = (out_ref.shape[1] - SAMPLE_ROWS) // PIECE
    for cube in range(CUBES):
        for at in range(pieces):
            out_ref[cube, at * PIECE : (at + 1) * PIECE, :] = near_ref[
                plan_ref[1 + at if pieces == STEPS else 5], cube * PIECE : (cube + 1) * PIECE, :
            ]
        out_ref[cube, pieces * PIECE :, :] = rows_ref[cube]


def assemble(pieces, plan, near, rows):
    return pl.pallas_call(
        assemble_kernel,
        out_shape=jax.ShapeDtypeStruct((CUBES, pieces * PIECE + SAMPLE_ROWS, LANES), jnp.bfloat16),
        in_specs=[pl.BlockSpec(memory_space=pltpu.SMEM)] + [pl.BlockSpec(memory_space=pltpu.VMEM)] * 2,
        out_specs=pl.BlockSpec(memory_space=pltpu.VMEM),
        compiler_params=vmem(8),
        cost_estimate=pl.CostEstimate(flops=1_000_000, bytes_accessed=2 << 20, transcendentals=0),
        name="assemble",
    )(plan, near, rows)


def line_up_kernel(plan_ref, received_ref, pieces_ref, out_ref, copies_ref, stage_ref, sem):
    count = (received_ref.shape[1] - SAMPLE_ROWS) // PIECE
    for step in range(STEPS):
        at = step * PIECE if count == STEPS else 0
        piece = received_ref[plan_ref[3 + step], at : at + PIECE, :]
        for cube in range(CUBES):
            copies_ref[cube, step * PIECE : (step + 1) * PIECE, :] = piece
    send = pltpu.make_async_copy(copies_ref, pieces_ref, sem)
    send.start()
    for cube in range(CUBES):
        stage_ref[cube * SAMPLE_ROWS : (cube + 1) * SAMPLE_ROWS, :] = received_ref[cube, count * PIECE :, :].astype(jnp.float32)
    for ch in range(STATION):
        for block in range(HALF_ROWS):
            rows = stage_ref[pl.ds(ch * HALF_ROWS + block, CUBES, stride=SAMPLE_ROWS), :]
            out_ref[ch * CUBES : (ch + 1) * CUBES, block * LANES : (block + 1) * LANES] = rows.astype(jnp.bfloat16)
    send.wait()


def line_up(plan, received):
    return pl.pallas_call(
        line_up_kernel,
        out_shape=[
            pltpu.HBM((CUBES, STEPS * PIECE, LANES), jnp.bfloat16),
            jax.ShapeDtypeStruct((CLASS_CH, HALF), jnp.bfloat16),
        ],
        in_specs=[pl.BlockSpec(memory_space=pltpu.SMEM), pl.BlockSpec(memory_space=pltpu.VMEM)],
        out_specs=[pl.BlockSpec(memory_space=pl.ANY), pl.BlockSpec(memory_space=pltpu.VMEM)],
        scratch_shapes=[
            pltpu.VMEM((CUBES, STEPS * PIECE, LANES), jnp.bfloat16),
            pltpu.VMEM((CUBES * SAMPLE_ROWS, LANES), jnp.float32),
            pltpu.SemaphoreType.DMA,
        ],
        compiler_params=vmem(8),
        cost_estimate=pl.CostEstimate(flops=1_000_000, bytes_accessed=2 << 20, transcendentals=0),
        name="line_up",
    )(plan, received)


def correlate_kernel(pieces_ref, *refs):
    *lines, out_ref, natural_ref, weight_ref, moved_ref, product_ref = refs
    bank = lax.axis_index("bank")
    own_run, own_half, klass = bank & 1, bank >> 1, class_of(lax.axis_index("group"))
    for quarter, line_ref in enumerate(lines):
        line = line_ref[...]
        for odd in range(2):
            for shift in range(SHIFTS):
                by = 16 * shift + 8 * odd
                at = odd * CH + shift * CLASS_CH
                moved_ref[quarter, at : at + CLASS_CH, :] = pltpu.roll(line, HALF - by, 1) if by else line
    for template in range(TPL):
        for step in range(STEPS):
            row = (template * STEPS + step) * 16
            for tile in range(CH // LANES):
                at = step * PIECE + tile * 16
                natural_ref[row : row + 16, tile * LANES : (tile + 1) * LANES] = pieces_ref[template, at : at + 16, :]
    wanted = iota((2 * ROWS, 1), 0)
    lag, step, template = wanted // 32, (wanted // 16) % 2, wanted % 16
    order = one_hot(iota((2 * ROWS, 2 * ROWS), 1) == (template * 2 + step) * 16 + lag)
    ordered = pltpu.roll(matmul(order, natural_ref[...]), (CH - klass * CLASS_CH) % CH, 1).astype(jnp.bfloat16)
    weight_ref[:, 0:CH] = ordered[0:ROWS]
    weight_ref[:, CH:] = ordered[ROWS:]
    for quarter in range(4):
        first = (own_run ^ (quarter >> 1)) * 4 + (own_half ^ (quarter & 1)) * 2
        for part, (start, stop) in enumerate(CHUNKS):
            product_ref[quarter, :, start:stop] = matmul(weight_ref[...], moved_ref[quarter, :, start:stop])
            at = part * TIME_DEV
            total = product_ref[quarter, 0:32, at : at + TIME_DEV]
            for lag in range(1, LAGS):
                window = product_ref[quarter, lag * 32 : (lag + 1) * 32, at : at + TIME_DEV + LANES]
                total = total + pltpu.roll(window, TIME_DEV + LANES - lag, 1)[:, :TIME_DEV]
            out_ref[first + part] = total


def correlate(pieces, *lines):
    return pl.pallas_call(
        correlate_kernel,
        out_shape=jax.ShapeDtypeStruct((CLASSES, STEPS * TPL, TIME_DEV), jnp.float32),
        in_specs=[pl.BlockSpec(memory_space=pltpu.VMEM)] * 5,
        out_specs=pl.BlockSpec(memory_space=pltpu.VMEM),
        scratch_shapes=[
            pltpu.VMEM((2 * ROWS, CH), jnp.bfloat16),
            pltpu.VMEM((ROWS, DEPTH), jnp.bfloat16),
            pltpu.VMEM((4, DEPTH, HALF), jnp.bfloat16),
            pltpu.VMEM((4, ROWS, HALF), jnp.float32),
        ],
        compiler_params=vmem(32),
        cost_estimate=pl.CostEstimate(flops=3_400_000_000, bytes_accessed=3 << 20, transcendentals=0),
        name="correlate",
    )(pieces, *lines)


def exchange(array, groups):
    return lax.all_to_all(array, "group", 0, 0, axis_index_groups=groups, tiled=True)


def body(traces, scales, templates, owners):
    station_ch, samples_all = traces.shape
    plan, by_class = split_block(owners.T, templates[0, 0])

    def sample_rows():
        blocked = traces.astype(jnp.float32).reshape(station_ch, scales.shape[1], -1)
        samples = (blocked * scales[:, :, None]).astype(jnp.bfloat16)
        return pack(samples.reshape(station_ch, samples_all // LANES, LANES))

    holds_owner, one_cube = (plan[0] & 1) == 1, plan[0] >= 2

    def from_cubes(count):
        def with_blocks():
            return assemble(count, plan, exchange(by_class, CUBE_GROUPS), sample_rows())

        def without_blocks():
            return jnp.pad(sample_rows(), ((0, 0), (count * PIECE, 0), (0, 0)))

        return line_up(plan, exchange(lax.cond(holds_owner, with_blocks, without_blocks), CLASS_GROUPS))

    piece, own = lax.cond(one_cube, lambda: from_cubes(2), lambda: from_cubes(1))
    halves, cores = [(0, 2), (2, 0), (1, 3), (3, 1)], [(0, 1), (1, 0), (2, 3), (3, 2)]
    other = lax.ppermute(own, "bank", halves)
    lines = [own, other, lax.ppermute(own, "bank", cores), lax.ppermute(other, "bank", cores)]
    pieces = exchange(piece, CLASS_GROUPS)
    partial = exchange(correlate(pieces, *lines), CUBE_GROUPS)
    scores = jnp.sum(partial, axis=0).reshape(STEPS, 1, TPL, TIME_DEV)
    best_score = lax.pmax(jnp.max(scores, axis=(0, 1, 2)), "bank")
    return (scores, best_score)


def solution(mesh):
    placed = (
        P("group", None),
        P("group", None),
        P("bank", "group", None, None, None),
        P(None, "bank"),
    )
    return jax.shard_map(
        body,
        mesh=mesh,
        in_specs=placed,
        out_specs=(P(None, "bank", None, "group"), P("group")),
        check_vma=False,
    )
```
